128 devices in a mesh: dp: 16 (over y, x_lo, core), seq: 8 (over z, x_hi).
Axes of the slice: x: 4 (x_hi: 2, x_lo: 2; x = x_hi * 2 + x_lo), y: 4, z: 4, core: 2. Of those that a mesh axis runs over, the one named last changes fastest.
Arguments:
- events: bfloat16 [16, 1024, 1024], P('dp', 'seq'), may hold values from -6 to 6
- in_weight: bfloat16 [1024, 4096], replicated, may hold values from -0.1875 to 0.1875
- out_weight: bfloat16 [1024, 1024], replicated, may hold values from -0.1875 to 0.1875
- rab_table: float32 [18, 8], replicated, may hold values from -4 to 4
- lengths: int32 [16, 4], P('dp'), may hold values from 1 to 512, 1024 in all within a row
- stamps: int32 [16, 1024], P('dp'), may hold values from 0 to 2096128, as said below
- cotangent: bfloat16 [16, 1024, 1024], P('dp', 'seq'), may hold values from -6 to 6
Outputs:
- layer_out: bfloat16 [16, 1024, 1024], P('dp', 'seq')
- input_grad: bfloat16 [16, 1024, 1024], P('dp', 'seq')
- out_weight_grad: float32 [1024, 1024], P(None, ('dp', 'seq'))
- bias_grad: float32 [18, 8], replicated
The draws below stay inside these ranges and needn't reach their ends.
Inputs may be any that keep to these rules, and one draw needn't show every extreme that they name: Each row holds 4 lengths that sum to 1024; the largest is exactly 512. `stamps`: each row never falls along the history positions, starts at 0 and ends at exactly 2096128.
All inputs are finite; a program needn't handle non-finite values.
Results may differ from the reference program's by a relative error of at most 0.017.
Values may be sent and summed in bfloat16 or wider, within the bound.
A program may use at most 128 MiB of HBM per device.

```python
import math
import jax
import jax.numpy as jnp
import numpy as np
from jax import lax

D = 1024
H = 8
TOK_DEV = 128
DOCS = 4
NB = 18
SEQLEN = 1024
BATCHES = 16
N_SEQ = 8


def draw_stamps(key, part):
    key = jax.random.fold_in(key, 11)
    key_scale, key_step = jax.random.split(key)
    exponents = jax.random.randint(key_scale, (BATCHES, SEQLEN), 0, 12)
    ceilings = jnp.left_shift(jnp.ones((BATCHES, SEQLEN), jnp.int32), exponents)
    steps_drawn = jax.random.randint(key_step, (BATCHES, SEQLEN), 0, ceilings)
    totals = jnp.cumsum(steps_drawn, axis=1)
    totals = totals - totals[:, :1]
    columns = jnp.arange(SEQLEN, dtype=jnp.int32)[None, :]
    final_stamp = jnp.full((BATCHES, SEQLEN), 2047 * SEQLEN, jnp.int32)
    return jnp.where(columns == SEQLEN - 1, final_stamp, totals)


def strengthened(values, own_key, source, target, blocks, factor):
    owner, partner = [(jnp.arange(values.shape[dim]) // (values.shape[dim] // blocks)).reshape([-1 if axis == dim else 1 for axis in range(values.ndim)]) for dim in (source, target)]
    chosen = jax.random.permutation(own_key, blocks)[partner]
    strong = (owner == chosen) | (owner == (partner + blocks // 2) % blocks)
    return jnp.where(strong, factor * values, values)


def steps_of(own_key, shape, pieces, smallest, high):
    def one(position, shards_of):
        heights = jax.random.uniform(jax.random.fold_in(jax.random.fold_in(own_key, 6), position), (shards_of,), jnp.float32, smallest / len(pieces), high / len(pieces))
        return jnp.repeat(jnp.exp(heights), shape[position] // shards_of).reshape((-1,) + (1,) * (len(shape) - position - 1))

    factor_of = one(*pieces[0])
    for cut in pieces[1:]:
        factor_of = factor_of * one(*cut)
    return factor_of


def length_profile(count, total, limit, lean):
    portions = [(1 << 20) // math.isqrt(rank ** lean) + 1 for rank in range(2, count + 1)]
    surplus, holding = total - limit - (count - 1), [1] * (count - 1)
    while surplus > 0:
        free = [i for i in range(count - 1) if holding[i] < limit]
        pool, remaining = sum([portions[i] for i in free]), surplus
        for i in free:
            extra = min(limit - holding[i], max(1, remaining * portions[i] // pool), surplus)
            holding[i] = holding[i] + extra
            surplus = surplus - extra
    return np.array([limit] + holding)


def ragged_sizes(stream_key, number_of, total, reach, slope):
    if number_of == 2:
        one = jax.random.randint(stream_key, (), max(1, total - reach), min(reach, total - 1) + 1)
        return jnp.stack([one, total - one])
    sizes = jnp.asarray(length_profile(number_of, total, reach, slope), jnp.int32)
    twos = (number_of - 1) // 2
    giver, receiver = sizes[1:1 + 2 * twos:2], sizes[2:2 + 2 * twos:2]
    slack = jnp.minimum(giver - 1, reach - receiver)
    moved = jax.random.randint(jax.random.fold_in(stream_key, 1), (twos,), 0, 1 << 20) % (slack + 1)
    sizes = sizes.at[1:1 + 2 * twos:2].set(giver - moved).at[2:2 + 2 * twos:2].set(receiver + moved)
    return sizes[jax.random.permutation(jax.random.fold_in(stream_key, 2), number_of)]


def gaussian(own_key, shape, width, most, shards=(), held_as=jnp.bfloat16):
    factor_of = steps_of(own_key, shape, shards, -0.22, 0.18) if shards else 1.0
    array = jax.random.normal(own_key, shape, jnp.float32) * width * factor_of
    return jnp.minimum(jnp.maximum(array, -most), most).astype(held_as)


def noise_with(rng, dims, width, bound, shards, heavy, held_as=jnp.bfloat16):
    result = width * jax.random.normal(rng, dims, jnp.float32)
    if shards:
        result = result * steps_of(rng, dims, shards, -0.22, 0.18)
    return jnp.clip(strengthened(result, jax.random.fold_in(rng, 3), *heavy), -bound, bound).astype(held_as)


def setup_inputs(seed: int = 0) -> dict:
    splits = jax.random.split(jax.random.key(seed), 8)
    return {
        "events": noise_with(splits[0], (BATCHES, SEQLEN, D), 1.0, 6.0, ((0, 16), (1, 8)), (1, 2, 8, 2.0)),
        "in_weight": gaussian(splits[1], (D, 4 * D), D ** -0.5, 0.1875),
        "out_weight": gaussian(splits[2], (D, D), D ** -0.5, 0.1875),
        "rab_table": gaussian(splits[3], (NB, H), 1.0, 4.0, (), jnp.float32),
        "lengths": jax.vmap(lambda own: ragged_sizes(own, DOCS, SEQLEN, SEQLEN // 2, 2))(jax.random.split(splits[4], BATCHES)).reshape((BATCHES, DOCS)).astype(jnp.int32),
        "stamps": draw_stamps(jax.random.fold_in(splits[7], 71), 0),
        "cotangent": noise_with(splits[6], (BATCHES, SEQLEN, D), 1.0, 6.0, ((0, 16), (1, 8)), (1, 2, 8, 2.0)),
    }


NORM_EPS = 1e-05

def silu_parts(values):
    sigmoid_v = jax.nn.sigmoid(values)
    return (values * sigmoid_v, sigmoid_v * (1.0 + values * (1.0 - sigmoid_v)))

def to_bf16(values):
    return lax.optimization_barrier(values.astype(jnp.bfloat16))

def row_positions(seq_len, rows_dev, shard_count):
    rows = jnp.arange(seq_len, dtype=jnp.int32)
    half_rows = rows_dev // 2
    shard = rows // rows_dev
    local = rows % rows_dev
    return jnp.where(local < half_rows, shard * half_rows + local, (2 * shard_count - 1 - shard) * half_rows + local - half_rows).astype(jnp.int32)

def one_batch(event_rows, lengths_row, stamps_row, cotangent_rows, in_weight, out_weight, rab_table):
    seq_len, width_all = event_rows.shape
    bucket_count, head_count = rab_table.shape
    head_size = width_all // head_count
    score_scale = 1.0 / head_size ** 0.5
    pre_act = jnp.dot(event_rows, in_weight, preferred_element_type=jnp.float32)
    activated, silu_slope = silu_parts(pre_act)
    activated_b = activated.astype(jnp.bfloat16)
    gate_rows = activated_b[:, :width_all]
    value_rows = activated_b[:, width_all:2 * width_all]
    query_rows = activated_b[:, 2 * width_all:3 * width_all]
    key_rows = activated_b[:, 3 * width_all:]
    positions = row_positions(seq_len, TOK_DEV, N_SEQ)
    doc_ends = jnp.cumsum(lengths_row)
    doc_ids = lax.optimization_barrier(jnp.sum((positions[:, None] >= doc_ends[None, :]).astype(jnp.int32), axis=1))
    visible = ((doc_ids[:, None] == doc_ids[None, :]) & (positions[None, :] <= positions[:, None])).astype(jnp.float32)
    row_stamps = jnp.take(stamps_row, positions)
    stamp_gap = row_stamps[:, None] - row_stamps[None, :]
    levels = 2 ** jnp.arange(bucket_count - 1, dtype=jnp.int32)
    bucket = lax.optimization_barrier(jnp.sum((stamp_gap[:, :, None] >= levels).astype(jnp.int32), axis=2))
    time_bias = jnp.transpose(rab_table[bucket], (2, 0, 1))
    query_heads = query_rows.astype(jnp.float32).reshape(seq_len, head_count, head_size)
    key_heads = key_rows.astype(jnp.float32).reshape(seq_len, head_count, head_size)
    value_heads = value_rows.astype(jnp.float32).reshape(seq_len, head_count, head_size)
    high = lax.Precision.HIGHEST
    scores = jnp.einsum('qhd,khd->hqk', query_heads, key_heads, precision=high) * score_scale + time_bias
    silu_s, slope_s = silu_parts(scores)
    probs_f = to_bf16(silu_s * visible[None]).astype(jnp.float32)
    attention = jnp.einsum('hqk,khd->qhd', probs_f, value_heads, precision=high).reshape(seq_len, width_all)
    centre = lax.optimization_barrier(jnp.mean(attention, axis=1, keepdims=True))
    centred = attention - centre
    sigma = jnp.sqrt(lax.optimization_barrier(jnp.mean(centred * centred, axis=1, keepdims=True)) + NORM_EPS)
    normed = centred / sigma
    gates_f = gate_rows.astype(jnp.float32)
    mixed = (normed * gates_f).astype(jnp.bfloat16)
    layer_out = jnp.dot(mixed, out_weight, preferred_element_type=jnp.float32).astype(jnp.bfloat16)
    grad_mixed = jnp.dot(cotangent_rows, out_weight.T, preferred_element_type=jnp.float32)
    grad_gate = grad_mixed * normed
    grad_normed = grad_mixed * gates_f
    grad_attn = (grad_normed - lax.optimization_barrier(jnp.mean(grad_normed, axis=1, keepdims=True)) - normed * lax.optimization_barrier(jnp.mean(grad_normed * normed, axis=1, keepdims=True))) / sigma
    grad_heads = to_bf16(grad_attn).astype(jnp.float32).reshape(seq_len, head_count, head_size)
    grad_probs = jnp.einsum('qhd,khd->hqk', grad_heads, value_heads, precision=high)
    grad_scores = grad_probs * visible[None] * slope_s
    grad_scores_f = to_bf16(grad_scores).astype(jnp.float32)
    grad_query = jnp.einsum('hqk,khd->qhd', grad_scores_f, key_heads, precision=high).reshape(seq_len, width_all) * score_scale
    grad_key = jnp.einsum('hqk,qhd->khd', grad_scores_f, query_heads, precision=high).reshape(seq_len, width_all) * score_scale
    grad_value = jnp.einsum('hqk,qhd->khd', probs_f, grad_heads, precision=high).reshape(seq_len, width_all)
    bias_term = jax.ops.segment_sum(jnp.transpose(grad_scores, (1, 2, 0)).reshape(-1, head_count), bucket.reshape(-1), num_segments=bucket_count)
    grad_pre = (jnp.concatenate([grad_gate, grad_value, grad_query, grad_key], axis=1) * silu_slope).astype(jnp.bfloat16)
    input_grad = jnp.dot(grad_pre, in_weight.T, preferred_element_type=jnp.float32).astype(jnp.bfloat16)
    out_term = jnp.dot(mixed.T, cotangent_rows, preferred_element_type=jnp.float32)
    return (layer_out, input_grad, out_term, bias_term)

def reference(events, in_weight, out_weight, rab_table, lengths, stamps, cotangent):

    def run_batch(items):
        return one_batch(items[0], items[1], items[2], items[3], in_weight, out_weight, rab_table)
    results = lax.map(run_batch, (events, lengths, stamps, cotangent))
    norm_scale = 1.0 / (events.shape[0] * events.shape[1]) ** 0.5
    return (results[0], results[1], lax.optimization_barrier(jnp.sum(results[2], axis=0)) * norm_scale, lax.optimization_barrier(jnp.sum(results[3], axis=0)) * norm_scale)
```

```python
import functools
import math

import jax
import jax.numpy as jnp
from jax import lax
from jax.experimental import pallas as pl
from jax.experimental.pallas import tpu as pltpu
from jax.sharding import PartitionSpec as P

NORM_EPS = 1e-05
HIDDEN = -1e30
MESH = pl.DeviceIdType.MESH
F32 = jnp.float32
BF16 = jnp.bfloat16

SEQ = 8
ROWS = 128
HALF = 64
LEN = 1024
WIDTH = 1024
HEAD = 128
BUCKETS = 18
STEP = 256


def dot(left, right):
    return jnp.dot(left, right, preferred_element_type=F32)


def dot_t(left, right):
    return lax.dot_general(left, right, (((1,), (1,)), ((), ())), preferred_element_type=F32)


def sigmoid(values):
    return 0.5 * jnp.tanh(0.5 * values) + 0.5


def aligned(value, multiple):
    return pl.multiple_of(value, multiple)


def kernel(
    events_ref,
    in_weight_ref,
    out_weight_ref,
    rab_ref,
    lengths_ref,
    stamps_ref,
    cot_ref,
    layer_out_ref,
    input_grad_ref,
    out_grad_ref,
    bias_grad_ref,
    w_qkv,
    w_gate,
    w_out,
    slope_qkv,
    slope_gate,
    gate_rows,
    grad_mixed,
    gn_rows,
    send_qkv,
    recv_qkv,
    recv_gn,
    query,
    key,
    value,
    gn_head,
    bias,
    bucket,
    slope,
    probs,
    dscores,
    attn,
    stat_send,
    stat_recv,
    normed_head,
    grad_attn,
    query_t,
    grad_attn_t,
    send_normed,
    recv_normed,
    dqkv_head,
    send_dqkv,
    recv_dqkv,
    mixed,
    gp_gate,
    ig_acc,
    cot_t,
    cot_t_other,
    part_own,
    part_send,
    part_recv,
    piece,
    piece_recv,
    hist,
    hist_recv,
    hist_sum,
    hist_all,
    load_sem,
    qkv_ss,
    qkv_rs,
    gn_ss,
    gn_rs,
    stat_ss,
    stat_rs,
    normed_ss,
    normed_rs,
    dqkv_ss,
    dqkv_rs,
    core_ss,
    core_rs,
    part_ss,
    part_rs,
    piece_ss,
    piece_rs,
    hist_ss,
    hist_rs,
    all_ss,
    all_rs,
):
    dp = lax.axis_index("dp")
    seq = lax.axis_index("seq")
    core = lax.rem(dp, 2)
    x_lo = lax.rem(dp // 2, 2)
    y = dp // 4
    other_core = 1 - core
    score_scale = 1.0 / HEAD**0.5
    norm_scale = 1.0 / math.sqrt(16 * LEN)

    def seq_peer(k):
        return (dp, lax.rem(seq + k + 1, SEQ))

    def seq_head(k):
        return lax.rem(seq + k + 1, SEQ)

    def y_index(k):
        return lax.rem(y + k + 1, 4)

    def y_peer(k):
        return (y_index(k) * 4 + lax.rem(dp, 4), seq)

    own_piece = x_lo * SEQ + seq

    def piece_index(k):
        return lax.rem(own_piece + k + 1, 16)

    def piece_peer(k):
        other = piece_index(k)
        return (y * 4 + (other // SEQ) * 2 + core, lax.rem(other, SEQ))

    def dp_peer(k):
        return (lax.rem(dp + k + 1, 16), seq)

    core_peer = (dp + 1 - 2 * core, seq)

    def remote(src, dst, ss, rs, device):
        return pltpu.make_async_remote_copy(
            src_ref=src,
            dst_ref=dst,
            send_sem=ss,
            recv_sem=rs,
            device_id=device,
            device_id_type=MESH,
        )

    events_copy = pltpu.make_async_copy(events_ref.at[0], mixed.at[1], load_sem.at[27])
    events_copy.start()

    def weight_copy(k, p):
        head = seq_head(k)
        return pltpu.make_async_copy(
            in_weight_ref.at[:, pl.ds(aligned((p + 1) * WIDTH + head * HEAD, HEAD), HEAD)],
            w_qkv.at[k, :, pl.ds(p * HEAD, HEAD)],
            load_sem.at[k * 3 + p],
        )

    for k in range(SEQ):
        for p in range(3):
            weight_copy(k, p).start()
    out_weight_copy = pltpu.make_async_copy(out_weight_ref, w_out, load_sem.at[24])
    out_weight_copy.start()
    gate_copy = pltpu.make_async_copy(
        in_weight_ref.at[:, pl.ds(0, WIDTH)], w_gate, load_sem.at[25]
    )
    gate_copy.start()

    barrier = pltpu.get_barrier_semaphore()

    def greet_piece(k, carry):
        pl.semaphore_signal(barrier, inc=1, device_id=piece_peer(k), device_id_type=MESH)
        return carry

    def greet_dp(k, carry):
        pl.semaphore_signal(barrier, inc=1, device_id=dp_peer(k), device_id_type=MESH)
        return carry

    lax.fori_loop(0, 15, greet_piece, 0)
    lax.fori_loop(0, 15, greet_dp, 0)

    events_copy.wait()
    pl.semaphore_wait(barrier, 30)

    def project(k):
        for p in range(3):
            weight_copy(k, p).wait()
        pre = dot(mixed[1], w_qkv[k])
        sig = sigmoid(pre)
        act = pre * sig
        slope_qkv[k] = sig + act * (1.0 - sig)
        return act.astype(BF16)

    def qkv_copy(k):
        return remote(
            send_qkv.at[k], recv_qkv.at[6 - k], qkv_ss.at[k], qkv_rs.at[6 - k], seq_peer(k)
        )

    def project_send(k, carry):
        send_qkv[k] = project(k)
        qkv_copy(k).start()
        return carry

    lax.fori_loop(0, 7, project_send, 0)
    recv_qkv[7] = project(7)

    out_weight_copy.wait()
    gate_copy.wait()
    for c in range(4):
        cols = pl.ds(c * STEP, STEP)
        pre = dot(mixed[1], w_gate[:, cols])
        sig = sigmoid(pre)
        act = pre * sig
        slope_gate[:, cols] = sig + act * (1.0 - sig)
        gate_b = act.astype(BF16)
        gate_rows[:, cols] = gate_b
        gm = dot_t(cot_ref[0], w_out[cols, :])
        grad_mixed[:, cols] = gm
        gn_rows[:, cols] = (gm * gate_b.astype(F32)).astype(BF16)

    def gn_copy(k):
        cols = pl.ds(aligned(seq_head(k) * HEAD, HEAD), HEAD)
        return remote(
            gn_rows.at[:, cols], recv_gn.at[6 - k], gn_ss.at[k], gn_rs.at[6 - k], seq_peer(k)
        )

    def send_gn(k, carry):
        gn_copy(k).start()
        return carry

    lax.fori_loop(0, 7, send_gn, 0)
    recv_gn[7] = gn_rows[:, pl.ds(aligned(seq * HEAD, HEAD), HEAD)]

    for g in range(8):
        tile = jnp.transpose(cot_ref[0, :, pl.ds(g * HEAD, HEAD)])
        cot_t[g, 0] = tile[:HALF]
        cot_t[g, 1] = tile[HALF:]
    cot_copy = remote(
        cot_t.at[:, other_core], cot_t_other, core_ss.at[0], core_rs.at[0], core_peer
    )
    cot_copy.start()

    lane = lax.broadcasted_iota(jnp.int32, (HEAD, HEAD), 1)
    sub = lax.broadcasted_iota(jnp.int32, (HEAD, HEAD), 0)
    table_bucket = jnp.minimum(32 - lane[:8], BUCKETS - 1)
    table = jnp.zeros((8, HEAD), F32)
    for b in range(BUCKETS):
        table = jnp.where(table_bucket == b, rab_ref[b, seq], table)
    table = jnp.broadcast_to(table[:1], (HEAD, HEAD))
    end_0 = lengths_ref[0, 0]
    end_1 = end_0 + lengths_ref[0, 1]
    end_2 = end_1 + lengths_ref[0, 2]
    for i in range(8):
        row_stamp = stamps_ref[:, pl.ds(i * HEAD, HEAD)].astype(F32)
        column_stamp = jnp.transpose(jnp.broadcast_to(row_stamp, (HEAD, HEAD))).astype(jnp.int32)
        row_pos = sub + i * HEAD
        first = jnp.where(
            row_pos >= end_2,
            end_2,
            jnp.where(row_pos >= end_1, end_1, jnp.where(row_pos >= end_0, end_0, 0)),
        )
        for j in range(2 * (i // 2) + 2):
            where = (pl.ds(i * HEAD, HEAD), pl.ds(j * HEAD, HEAD))
            key_pos = lane + j * HEAD
            leading = lax.clz(column_stamp - stamps_ref[:, pl.ds(j * HEAD, HEAD)])
            visible = (key_pos >= first) & (key_pos <= row_pos)
            bias[where] = jnp.where(
                visible, jnp.take_along_axis(table, leading, axis=1), HIDDEN
            )
            bucket[where] = jnp.minimum(32 - leading, BUCKETS - 1)

    def halves(block):
        return (
            pl.ds(aligned(block * HALF, HALF), HALF),
            pl.ds(aligned(LEN - HALF - block * HALF, HALF), HALF),
        )

    def place_qkv(j):
        low, high = halves(seq_head(j))
        for at, rows in ((low, slice(0, HALF)), (high, slice(HALF, ROWS))):
            for p, target in enumerate((value, query, key)):
                target[at, :] = recv_qkv[j, rows, p * HEAD : (p + 1) * HEAD]

    def take_qkv(j, carry):
        qkv_copy(6 - j).wait_recv()
        place_qkv(j)
        return carry

    place_qkv(7)
    lax.fori_loop(0, 7, take_qkv, 0)

    def place_gn(j):
        low, high = halves(seq_head(j))
        gn_head[low, :] = recv_gn[j, :HALF]
        gn_head[high, :] = recv_gn[j, HALF:]

    def take_gn(j, carry):
        gn_copy(6 - j).wait_recv()
        place_gn(j)
        return carry

    for i in range(4):
        rows = pl.ds(i * STEP, STEP)
        for j in range(i + 1):
            cols = pl.ds(j * STEP, STEP)
            scores = dot_t(query[rows, :], key[cols, :]) * score_scale + bias[rows, cols]
            sig = sigmoid(scores)
            silu = scores * sig
            probs[rows, cols] = silu.astype(BF16)
            slope[rows, cols] = sig + silu * (1.0 - sig)
        seen = (i + 1) * STEP
        attn[rows, :] = dot(probs[rows, :seen], value[:seen, :])

    place_gn(7)
    lax.fori_loop(0, 7, take_gn, 0)

    def column_stats(i):
        rows = pl.ds(i * HEAD, HEAD)
        a = attn[rows, :]
        g = gn_head[rows, :].astype(F32)
        mean = jnp.mean(a, axis=1, keepdims=True)
        off = a - mean
        return (
            mean,
            jnp.sum(off * off, axis=1, keepdims=True),
            jnp.sum(g * off, axis=1, keepdims=True),
            jnp.sum(g, axis=1, keepdims=True),
        )

    for i in range(4):
        packed = jnp.zeros((HEAD, HEAD), F32)
        for n, column in enumerate(column_stats(i) + column_stats(i + 4)):
            packed = jnp.where(lane == n, column, packed)
        stat_send[:, pl.ds(i * HEAD, HEAD)] = jnp.transpose(packed)[:8]

    def stat_copy(k):
        return remote(
            stat_send, stat_recv.at[6 - k], stat_ss.at[k], stat_rs.at[6 - k], seq_peer(k)
        )

    def send_stat(k, carry):
        stat_copy(k).start()
        return carry

    lax.fori_loop(0, 7, send_stat, 0)
    stat_recv[7] = stat_send[...]
    for i in range(8):
        rows = pl.ds(i * HEAD, HEAD)
        query_t[:, rows] = jnp.transpose(query[rows, :])

    def take_stat(j, carry):
        stat_copy(6 - j).wait_recv()
        return carry

    lax.fori_loop(0, 7, take_stat, 0)

    for part in range(2):
        rows4 = [[stat_recv[j, part * 4 + n : part * 4 + n + 1, :] for n in range(4)] for j in range(SEQ)]
        mu = sum(r[0] for r in rows4) * (1.0 / SEQ)
        spread = sum(r[1] + HEAD * (r[0] - mu) * (r[0] - mu) for r in rows4)
        inverse = 1.0 / jnp.sqrt(spread * (1.0 / WIDTH) + NORM_EPS)
        along = sum(r[2] + (r[0] - mu) * r[3] for r in rows4) * inverse * (1.0 / WIDTH)
        level = sum(r[3] for r in rows4) * (1.0 / WIDTH)
        for i in range(4):
            at = slice(i * HEAD, (i + 1) * HEAD)
            tile = jnp.where(
                sub == 0,
                mu[:, at],
                jnp.where(sub == 1, inverse[:, at], jnp.where(sub == 2, along[:, at], level[:, at])),
            )
            tile = jnp.transpose(tile)
            rows = pl.ds((part * 4 + i) * HEAD, HEAD)
            normed = (attn[rows, :] - tile[:, 0:1]) * tile[:, 1:2]
            normed_head[rows, :] = normed.astype(BF16)
            grad_attn[rows, :] = (
                (gn_head[rows, :].astype(F32) - tile[:, 3:4] - normed * tile[:, 2:3]) * tile[:, 1:2]
            ).astype(BF16)

    def normed_copy(k):
        return remote(
            send_normed.at[k],
            recv_normed.at[6 - k],
            normed_ss.at[k],
            normed_rs.at[6 - k],
            seq_peer(k),
        )

    def pick_normed(k, target):
        low, high = halves(seq_head(k))
        target[k, :HALF] = normed_head[low, :]
        target[k, HALF:] = normed_head[high, :]

    def send_norm(k, carry):
        pick_normed(k, send_normed)
        normed_copy(k).start()
        return carry

    lax.fori_loop(0, 7, send_norm, 0)
    pick_normed(7, recv_normed)

    for i in range(8):
        rows = pl.ds(i * HEAD, HEAD)
        grad_attn_t[:, rows] = jnp.transpose(grad_attn[rows, :])
    for i in range(4):
        rows = pl.ds(i * STEP, STEP)
        for j in range(i + 1):
            cols = pl.ds(j * STEP, STEP)
            ds = dot_t(grad_attn[rows, :], value[cols, :]) * slope[rows, cols]
            slope[rows, cols] = ds
            dscores[rows, cols] = ds.astype(BF16)
        seen = (i + 1) * STEP
        dqkv_head[rows, HEAD : 2 * HEAD] = (
            dot(dscores[rows, :seen], key[:seen, :]) * score_scale
        ).astype(BF16)
    for j in range(4):
        cols = pl.ds(j * STEP, STEP)
        rest = slice(j * STEP, LEN)
        grad_value = dot(grad_attn_t[:, rest], probs[rest, cols])
        grad_key = dot(query_t[:, rest], dscores[rest, cols]) * score_scale
        dqkv_head[cols, 0:HEAD] = jnp.transpose(grad_value).astype(BF16)
        dqkv_head[cols, 2 * HEAD : 3 * HEAD] = jnp.transpose(grad_key).astype(BF16)

    def dqkv_copy(k):
        return remote(
            send_dqkv.at[k], recv_dqkv.at[6 - k], dqkv_ss.at[k], dqkv_rs.at[6 - k], seq_peer(k)
        )

    def pick_dqkv(k, target):
        low, high = halves(seq_head(k))
        target[k, :HALF] = dqkv_head[low, :]
        target[k, HALF:] = dqkv_head[high, :]

    def send_grad(k, carry):
        pick_dqkv(k, send_dqkv)
        dqkv_copy(k).start()
        return carry

    lax.fori_loop(0, 7, send_grad, 0)
    pick_dqkv(7, recv_dqkv)

    def rows_of_head(j):
        cols = pl.ds(aligned(seq_head(j) * HEAD, HEAD), HEAD)
        normed = recv_normed[j].astype(F32)
        mixed[0, :, cols] = (normed * gate_rows[:, cols].astype(F32)).astype(BF16)
        gp_gate[:, cols] = (grad_mixed[:, cols] * normed * slope_gate[:, cols]).astype(BF16)

    def take_normed(j, carry):
        normed_copy(6 - j).wait_recv()
        rows_of_head(j)
        return carry

    rows_of_head(7)
    lax.fori_loop(0, 7, take_normed, 0)

    ready = remote(
        mixed.at[0], mixed_other_ref(mixed), core_ss.at[1], core_rs.at[1], core_peer
    )
    ready.start()
    for c in range(4):
        cols = pl.ds(c * STEP, STEP)
        layer_out_ref[0, :, cols] = dot(mixed[0], w_out[:, cols]).astype(BF16)
        ig_acc[:, cols] = dot_t(gp_gate[...], w_gate[cols, :])

    cot_copy.wait_recv()
    ready.wait_recv()
    both = mixed_pair(mixed)

    def part_copy(k):
        return remote(
            part_send.at[k], part_recv.at[2 - k], part_ss.at[k], part_rs.at[2 - k], y_peer(k)
        )

    def part_rows(k):
        group = y_index(k) * 2
        left = jnp.concatenate(
            [
                jnp.concatenate([cot_t[group, core], cot_t[group + 1, core]], axis=0),
                jnp.concatenate([cot_t_other[group], cot_t_other[group + 1]], axis=0),
            ],
            axis=1,
        )
        return left

    for k in range(4):
        left = part_rows(k)
        for c in range(4):
            cols = slice(c * STEP, (c + 1) * STEP)
            product = dot(left, both[:, cols])
            if k < 3:
                part_send[k, :, cols] = product.astype(BF16)
            else:
                part_own[:, cols] = product
        if k < 3:
            part_copy(k).start()

    for i in range(4):

        def add_rows(r, sums):
            rows = pl.ds(aligned(i * STEP + r * 8, 8), 8)
            for j in range(2 * (i + 1)):
                cols = pl.ds(j * HEAD, HEAD)
                ds = slope[rows, cols]
                which = bucket[rows, cols]
                sums = tuple(
                    total + jnp.where(which == b, ds, 0.0) for b, total in enumerate(sums)
                )
            return sums

        zeros = tuple(jnp.zeros((8, HEAD), F32) for _ in range(BUCKETS))
        sums = lax.fori_loop(0, STEP // 8, add_rows, zeros if i == 0 else sums)
    hist[...] = jnp.zeros((24, HEAD), F32)
    for b in range(BUCKETS):
        hist[b : b + 1, :] = jnp.sum(sums[b], axis=0, keepdims=True)

    def hist_copy(k):
        return remote(hist, hist_recv.at[14 - k], hist_ss.at[k], hist_rs.at[14 - k], dp_peer(k))

    def send_hist(k, carry):
        hist_copy(k).start()
        return carry

    lax.fori_loop(0, 15, send_hist, 0)

    for k in range(3):
        part_copy(k).wait_recv()
    for g in range(2):
        for c in range(8):
            rows = slice(g * HALF + c * 8, g * HALF + c * 8 + 8)
            total = part_own[rows, :]
            for k in range(3):
                base = g * HALF + (c // 2) * 16
                pair = part_recv[k, base : base + 16, :].astype(F32)
                total = total + pair[(c % 2) * 8 : (c % 2) * 8 + 8]
            piece[g * 8 + c] = jnp.concatenate(
                [total[:, : WIDTH // 2], total[:, WIDTH // 2 :]], axis=0
            ).astype(BF16)

    def piece_copy(k):
        return remote(
            piece.at[piece_index(k)],
            piece_recv.at[14 - k],
            piece_ss.at[k],
            piece_rs.at[14 - k],
            piece_peer(k),
        )

    def send_piece(k, carry):
        piece_copy(k).start()
        return carry

    lax.fori_loop(0, 15, send_piece, 0)

    def take_hist(k, total):
        hist_copy(14 - k).wait_recv()
        return total + hist_recv[k]

    hist_sum[...] = lax.fori_loop(0, 15, take_hist, hist[...]) * norm_scale

    def all_copy(k):
        return remote(hist_sum, hist_all.at[6 - k], all_ss.at[k], all_rs.at[6 - k], seq_peer(k))

    def send_all(k, carry):
        all_copy(k).start()
        return carry

    lax.fori_loop(0, 7, send_all, 0)

    def add_head(j):
        grad_pre = (recv_dqkv[j].astype(F32) * slope_qkv[j]).astype(BF16)
        for c in range(4):
            cols = pl.ds(c * STEP, STEP)
            ig_acc[:, cols] += dot_t(grad_pre, w_qkv[j, cols, :])

    def take_dqkv(j, carry):
        dqkv_copy(6 - j).wait_recv()
        add_head(j)
        return carry

    add_head(7)
    lax.fori_loop(0, 7, take_dqkv, 0)
    input_grad_ref[0] = ig_acc[...].astype(BF16)

    def take_piece(k, total):
        piece_copy(14 - k).wait_recv()
        return total + piece_recv[k].astype(F32)

    total = lax.fori_loop(0, 15, take_piece, piece[own_piece].astype(F32)) * norm_scale
    out_grad_ref[:, : WIDTH // 2] = total[:8]
    out_grad_ref[:, WIDTH // 2 :] = total[8:]

    def head_column(j, table):
        column = jnp.sum(hist_all[j], axis=1, keepdims=True)
        return jnp.where(lane[:24] == seq_head(j), column, table)

    hist_all[7] = hist_sum[...]

    def take_all(j, table):
        all_copy(6 - j).wait_recv()
        return head_column(j, table)

    table = head_column(7, jnp.zeros((24, HEAD), F32))
    bias_grad_ref[...] = lax.fori_loop(0, 7, take_all, table)

    def sent_seq(k, carry):
        for copy in (qkv_copy, gn_copy, stat_copy, normed_copy, dqkv_copy, all_copy):
            copy(k).wait_send()
        return carry

    def sent_many(k, carry):
        piece_copy(k).wait_send()
        hist_copy(k).wait_send()
        return carry

    lax.fori_loop(0, 7, sent_seq, 0)
    lax.fori_loop(0, 15, sent_many, 0)
    for k in range(3):
        part_copy(k).wait_send()
    cot_copy.wait_send()
    ready.wait_send()


def mixed_other_ref(mixed):
    return mixed.at[2]


def mixed_pair(mixed):
    return jnp.concatenate([mixed[0], mixed[2]], axis=0)


def body(events, in_weight, out_weight, rab_table, lengths, stamps, cotangent):
    dma = pltpu.SemaphoreType.DMA
    vmem = pltpu.VMEM
    scratch = [
        vmem((SEQ, WIDTH, 3 * HEAD), BF16),
        vmem((WIDTH, WIDTH), BF16),
        vmem((WIDTH, WIDTH), BF16),
        vmem((SEQ, ROWS, 3 * HEAD), F32),
        vmem((ROWS, WIDTH), F32),
        vmem((ROWS, WIDTH), BF16),
        vmem((ROWS, WIDTH), F32),
        vmem((ROWS, WIDTH), BF16),
        vmem((SEQ, ROWS, 3 * HEAD), BF16),
        vmem((SEQ, ROWS, 3 * HEAD), BF16),
        vmem((SEQ, ROWS, HEAD), BF16),
        vmem((LEN, HEAD), BF16),
        vmem((LEN, HEAD), BF16),
        vmem((LEN, HEAD), BF16),
        vmem((LEN, HEAD), BF16),
        vmem((LEN, LEN), F32),
        vmem((LEN, LEN), jnp.int32),
        vmem((LEN, LEN), F32),
        vmem((LEN, LEN), BF16),
        vmem((LEN, LEN), BF16),
        vmem((LEN, HEAD), F32),
        vmem((8, LEN // 2), F32),
        vmem((SEQ, 8, LEN // 2), F32),
        vmem((LEN, HEAD), BF16),
        vmem((LEN, HEAD), BF16),
        vmem((HEAD, LEN), BF16),
        vmem((HEAD, LEN), BF16),
        vmem((SEQ, ROWS, HEAD), BF16),
        vmem((SEQ, ROWS, HEAD), BF16),
        vmem((LEN, 3 * HEAD), BF16),
        vmem((SEQ, ROWS, 3 * HEAD), BF16),
        vmem((SEQ, ROWS, 3 * HEAD), BF16),
        vmem((3, ROWS, WIDTH), BF16),
        vmem((ROWS, WIDTH), BF16),
        vmem((ROWS, WIDTH), F32),
        vmem((8, 2, HALF, ROWS), BF16),
        vmem((8, HALF, ROWS), BF16),
        vmem((ROWS, WIDTH), F32),
        vmem((3, ROWS, WIDTH), BF16),
        vmem((3, ROWS, WIDTH), BF16),
        vmem((16, 16, WIDTH // 2), BF16),
        vmem((15, 16, WIDTH // 2), BF16),
        vmem((24, HEAD), F32),
        vmem((15, 24, HEAD), F32),
        vmem((24, HEAD), F32),
        vmem((SEQ, 24, HEAD), F32),
        dma((28,)),
        dma((7,)),
        dma((7,)),
        dma((7,)),
        dma((7,)),
        dma((7,)),
        dma((7,)),
        dma((7,)),
        dma((7,)),
        dma((7,)),
        dma((7,)),
        dma((2,)),
        dma((2,)),
        dma((3,)),
        dma((3,)),
        dma((15,)),
        dma((15,)),
        dma((15,)),
        dma((15,)),
        dma((7,)),
        dma((7,)),
    ]
    hbm = pl.BlockSpec(memory_space=pl.ANY)
    local = pl.BlockSpec(memory_space=pltpu.VMEM)
    scalar = pl.BlockSpec(memory_space=pltpu.SMEM)
    layer_out, input_grad, out_grad, bias_grad = pl.pallas_call(
        kernel,
        out_shape=(
            jax.ShapeDtypeStruct((1, ROWS, WIDTH), BF16),
            jax.ShapeDtypeStruct((1, ROWS, WIDTH), BF16),
            jax.ShapeDtypeStruct((8, WIDTH), F32),
            jax.ShapeDtypeStruct((24, HEAD), F32),
        ),
        in_specs=[hbm, hbm, hbm, scalar, scalar, local, local],
        out_specs=(local,) * 4,
        scratch_shapes=scratch,
        compiler_params=pltpu.CompilerParams(
            collective_id=0, has_side_effects=True, vmem_limit_bytes=60 * 2**20
        ),
    )(events, in_weight, out_weight, rab_table, lengths, stamps, cotangent)
    return (layer_out, input_grad, out_grad.T, bias_grad[:BUCKETS, : rab_table.shape[1]])


def solution(mesh):
    placed = (
        P("dp", "seq", None),
        P(),
        P(),
        P(),
        P("dp", None),
        P("dp", None),
        P("dp", "seq", None),
    )
    return jax.shard_map(
        body,
        mesh=mesh,
        in_specs=placed,
        out_specs=(P("dp", "seq", None), P("dp", "seq", None), P(None, ("dp", "seq")), P()),
        check_vma=False,
    )
```

```python
import functools
import math

import jax
import jax.numpy as jnp
from jax import lax
from jax.experimental import pallas as pl
from jax.experimental.pallas import tpu as pltpu
from jax.sharding import PartitionSpec as P

NORM_EPS = 1e-05
HIDDEN = -1e30
MESH = pl.DeviceIdType.MESH
F32 = jnp.float32
BF16 = jnp.bfloat16

SEQ = 8
ROWS = 128
HALF = 64
LEN = 1024
WIDTH = 1024
HEAD = 128
BUCKETS = 18
STEP = 256


def dot(left, right):
    return jnp.dot(left, right, preferred_element_type=F32)


def dot_t(left, right):
    return lax.dot_general(left, right, (((1,), (1,)), ((), ())), preferred_element_type=F32)


def sigmoid(values):
    return 0.5 * jnp.tanh(0.5 * values) + 0.5


def aligned(value, multiple):
    return pl.multiple_of(value, multiple)


def kernel(
    events_ref,
    in_weight_ref,
    out_weight_ref,
    rab_ref,
    lengths_ref,
    stamps_ref,
    cot_ref,
    layer_out_ref,
    input_grad_ref,
    out_grad_ref,
    bias_grad_ref,
    w_qkv,
    w_gate,
    w_out,
    slope_qkv,
    slope_gate,
    gate_rows,
    grad_mixed,
    gn_rows,
    send_qkv,
    recv_qkv,
    recv_gn,
    query,
    key,
    value,
    gn_head,
    bias,
    bucket,
    slope,
    probs,
    dscores,
    attn,
    stat_send,
    stat_recv,
    normed_head,
    grad_attn,
    query_t,
    grad_attn_t,
    send_normed,
    recv_normed,
    dqkv_head,
    send_dqkv,
    recv_dqkv,
    event_rows,
    mixed,
    gp_gate,
    ig_acc,
    cot_all,
    mixed_all,
    mixed_t,
    piece,
    piece_recv,
    final_send,
    final_recv,
    hist,
    hist_recv,
    hist_sum,
    hist_all,
    rab,
    lengths,
    stamps,
    layer_out_rows,
    input_grad_rows,
    store_sem,
    small_sem,
    load_sem,
    qkv_ss,
    qkv_rs,
    gn_ss,
    gn_rs,
    stat_ss,
    stat_rs,
    normed_ss,
    normed_rs,
    dqkv_ss,
    dqkv_rs,
    cot_ss,
    cot_rs,
    core_ss,
    core_rs,
    mixed_ss,
    mixed_rs,
    final_ss,
    final_rs,
    piece_ss,
    piece_rs,
    hist_ss,
    hist_rs,
    all_ss,
    all_rs,
):
    dp = lax.axis_index("dp")
    seq = lax.axis_index("seq")
    core = lax.rem(dp, 2)
    x_lo = lax.rem(dp // 2, 2)
    y = dp // 4
    score_scale = 1.0 / HEAD**0.5
    norm_scale = 1.0 / math.sqrt(16 * LEN)

    def seq_head(k):
        along_z = lax.rem(seq // 2 + k - 3 * (k // 4), 4)
        return along_z * 2 + lax.rem(seq + k + 1, 2)

    def seq_peer(k):
        return (dp, seq_head(k))

    def back(k):
        upper = k // 4
        return (1 - upper) * lax.rem(8 - k, 4) + upper * (10 - k)

    def y_peer(k):
        return (lax.rem(y + k + 1, 4) * 4 + lax.rem(dp, 4), seq)

    own_group = y * 2 + core

    def group_index(k):
        return lax.rem(own_group + k + 1, 8)

    def group_peer(k):
        other = group_index(k)
        return ((other // 2) * 4 + x_lo * 2 + lax.rem(other, 2), seq)

    own_piece = x_lo * SEQ + seq

    def piece_index(k):
        return lax.rem(own_piece + k + 1, 16)

    def piece_peer(k):
        other = piece_index(k)
        return (y * 4 + (other // SEQ) * 2 + core, lax.rem(other, SEQ))

    def dp_peer(k):
        return (lax.rem(dp + k + 1, 16), seq)

    core_peer = (dp + 1 - 2 * core, seq)

    def remote(src, dst, ss, rs, device):
        return pltpu.make_async_remote_copy(
            src_ref=src,
            dst_ref=dst,
            send_sem=ss,
            recv_sem=rs,
            device_id=device,
            device_id_type=MESH,
        )

    events_copy = pltpu.make_async_copy(events_ref.at[0], event_rows, load_sem.at[27])
    events_copy.start()

    small_copies = [
        pltpu.make_async_copy(source, target, small_sem.at[n])
        for n, (source, target) in enumerate(
            ((rab_ref, rab), (lengths_ref, lengths), (stamps_ref, stamps))
        )
    ]
    for copy in small_copies:
        copy.start()

    barrier = pltpu.get_barrier_semaphore()

    def greet_piece(k, carry):
        pl.semaphore_signal(barrier, inc=1, device_id=piece_peer(k), device_id_type=MESH)
        return carry

    def greet_dp(k, carry):
        pl.semaphore_signal(barrier, inc=1, device_id=dp_peer(k), device_id_type=MESH)
        return carry

    lax.fori_loop(0, 15, greet_piece, 0)
    lax.fori_loop(0, 15, greet_dp, 0)

    def weight_copy(k, p):
        head = seq_head(k)
        return pltpu.make_async_copy(
            in_weight_ref.at[:, pl.ds(aligned((p + 1) * WIDTH + head * HEAD, HEAD), HEAD)],
            w_qkv.at[k, :, pl.ds(p * HEAD, HEAD)],
            load_sem.at[k * 3 + p],
        )

    for k in range(SEQ):
        for p in range(3):
            weight_copy(k, p).start()
    out_weight_copy = pltpu.make_async_copy(out_weight_ref, w_out, load_sem.at[24])
    out_weight_copy.start()
    gate_copy = pltpu.make_async_copy(
        in_weight_ref.at[:, pl.ds(0, WIDTH)], w_gate, load_sem.at[25]
    )
    gate_copy.start()
    cot_load = pltpu.make_async_copy(cot_ref.at[0], cot_all.at[own_group], load_sem.at[26])
    cot_load.start()

    events_copy.wait()

    def project(k):
        for p in range(3):
            weight_copy(k, p).wait()
        pre = dot(event_rows[...], w_qkv[k])
        sig = sigmoid(pre)
        act = pre * sig
        slope_qkv[k] = sig + act * (1.0 - sig)
        return act.astype(BF16)

    def qkv_copy(k):
        return remote(
            send_qkv.at[k], recv_qkv.at[back(k)], qkv_ss.at[k], qkv_rs.at[back(k)], seq_peer(k)
        )

    def project_keep(k, carry):
        send_qkv[k] = project(k)
        return carry

    def project_send(k, carry):
        send_qkv[k] = project(k)
        qkv_copy(k).start()
        return carry

    def send_kept(k, carry):
        qkv_copy(k).start()
        return carry

    lax.fori_loop(0, 1, project_keep, 0)
    pl.semaphore_wait(barrier, 30)
    lax.fori_loop(0, 1, send_kept, 0)
    lax.fori_loop(1, 5, project_send, 0)
    lax.fori_loop(5, 7, project_keep, 0)
    recv_qkv[7] = project(7)
    qkv_copy(0).wait_send()
    qkv_copy(5).start()

    out_weight_copy.wait()
    gate_copy.wait()
    cot_load.wait()
    for c in range(4):
        cols = pl.ds(c * STEP, STEP)
        pre = dot(event_rows[...], w_gate[:, cols])
        sig = sigmoid(pre)
        act = pre * sig
        slope_gate[:, cols] = sig + act * (1.0 - sig)
        gate_b = act.astype(BF16)
        gate_rows[:, cols] = gate_b
        gm = dot_t(cot_all[own_group], w_out[cols, :])
        grad_mixed[:, cols] = gm
        gn_rows[:, cols] = (gm * gate_b.astype(F32)).astype(BF16)

    def gn_copy(k):
        cols = pl.ds(aligned(seq_head(k) * HEAD, HEAD), HEAD)
        return remote(
            gn_rows.at[:, cols], recv_gn.at[back(k)], gn_ss.at[k], gn_rs.at[back(k)], seq_peer(k)
        )

    def send_gn(k, carry):
        gn_copy(k).start()
        return carry

    recv_gn[7] = gn_rows[:, pl.ds(aligned(seq * HEAD, HEAD), HEAD)]
    qkv_copy(1).wait_send()
    qkv_copy(6).start()

    def cot_copy(k):
        return remote(
            cot_all.at[own_group], cot_all.at[own_group], cot_ss.at[k], cot_rs.at[2 - k], y_peer(k)
        )

    def send_cot(k, carry):
        cot_copy(k).start()
        return carry

    lane = lax.broadcasted_iota(jnp.int32, (HEAD, HEAD), 1)
    sub = lax.broadcasted_iota(jnp.int32, (HEAD, HEAD), 0)
    for copy in small_copies:
        copy.wait()
    table_bucket = jnp.minimum(32 - lane[:8], BUCKETS - 1)
    table = jnp.zeros((8, HEAD), F32)
    for b in range(BUCKETS):
        table = jnp.where(table_bucket == b, rab[seq, b], table)
    table = jnp.broadcast_to(table[:1], (HEAD, HEAD))
    end_0 = lengths[0, 0]
    end_1 = end_0 + lengths[0, 1]
    end_2 = end_1 + lengths[0, 2]
    for i in range(8):
        row_stamp = stamps[:, pl.ds(i * HEAD, HEAD)].astype(F32)
        column_stamp = jnp.transpose(jnp.broadcast_to(row_stamp, (HEAD, HEAD))).astype(jnp.int32)
        row_pos = sub + i * HEAD
        first = jnp.where(
            row_pos >= end_2,
            end_2,
            jnp.where(row_pos >= end_1, end_1, jnp.where(row_pos >= end_0, end_0, 0)),
        )
        for j in range(2 * (i // 2) + 2):
            where = (pl.ds(i * HEAD, HEAD), pl.ds(j * HEAD, HEAD))
            key_pos = lane + j * HEAD
            leading = lax.clz(column_stamp - stamps[:, pl.ds(j * HEAD, HEAD)])
            visible = (key_pos >= first) & (key_pos <= row_pos)
            bias[where] = jnp.where(
                visible, jnp.take_along_axis(table, leading, axis=1), HIDDEN
            )
            bucket[where] = jnp.minimum(32 - leading, BUCKETS - 1)

    def halves(block):
        return (
            pl.ds(aligned(block * HALF, HALF), HALF),
            pl.ds(aligned(LEN - HALF - block * HALF, HALF), HALF),
        )

    def place_qkv(j):
        low, high = halves(seq_head(j))
        for at, rows in ((low, slice(0, HALF)), (high, slice(HALF, ROWS))):
            for p, target in enumerate((value, query, key)):
                target[at, :] = recv_qkv[j, rows, p * HEAD : (p + 1) * HEAD]

    def take_qkv(j, carry):
        qkv_copy(back(j)).wait_recv()
        place_qkv(j)
        return carry

    place_qkv(7)
    qkv_copy(2).wait_send()
    qkv_copy(3).wait_send()
    lax.fori_loop(0, 7, send_gn, 0)
    lax.fori_loop(0, 3, send_cot, 0)
    lax.fori_loop(0, 7, take_qkv, 0)

    def place_gn(j):
        low, high = halves(seq_head(j))
        gn_head[low, :] = recv_gn[j, :HALF]
        gn_head[high, :] = recv_gn[j, HALF:]

    def take_gn(j, carry):
        gn_copy(back(j)).wait_recv()
        place_gn(j)
        return carry

    for i in range(4):
        rows = pl.ds(i * STEP, STEP)
        for j in range(i + 1):
            cols = pl.ds(j * STEP, STEP)
            scores = dot_t(query[rows, :], key[cols, :]) * score_scale + bias[rows, cols]
            sig = sigmoid(scores)
            silu = scores * sig
            probs[rows, cols] = silu.astype(BF16)
            slope[rows, cols] = sig + silu * (1.0 - sig)
        seen = (i + 1) * STEP
        attn[rows, :] = dot(probs[rows, :seen], value[:seen, :])

    place_gn(7)
    lax.fori_loop(0, 7, take_gn, 0)

    def column_stats(i):
        rows = pl.ds(i * HEAD, HEAD)
        a = attn[rows, :]
        g = gn_head[rows, :].astype(F32)
        mean = jnp.mean(a, axis=1, keepdims=True)
        off = a - mean
        return (
            mean,
            jnp.sum(off * off, axis=1, keepdims=True),
            jnp.sum(g * off, axis=1, keepdims=True),
            jnp.sum(g, axis=1, keepdims=True),
        )

    for i in range(4):
        packed = jnp.zeros((HEAD, HEAD), F32)
        for n, column in enumerate(column_stats(i) + column_stats(i + 4)):
            packed = jnp.where(lane == n, column, packed)
        stat_send[:, pl.ds(i * HEAD, HEAD)] = jnp.transpose(packed)[:8]

    def stat_copy(k):
        return remote(
            stat_send, stat_recv.at[back(k)], stat_ss.at[k], stat_rs.at[back(k)], seq_peer(k)
        )

    def send_stat(k, carry):
        stat_copy(k).start()
        return carry

    lax.fori_loop(0, 7, send_stat, 0)
    stat_recv[7] = stat_send[...]
    for i in range(8):
        rows = pl.ds(i * HEAD, HEAD)
        query_t[:, rows] = jnp.transpose(query[rows, :])

    def take_stat(j, carry):
        stat_copy(back(j)).wait_recv()
        return carry

    lax.fori_loop(0, 7, take_stat, 0)

    for part in range(2):
        rows4 = [[stat_recv[j, part * 4 + n : part * 4 + n + 1, :] for n in range(4)] for j in range(SEQ)]
        mu = sum(r[0] for r in rows4) * (1.0 / SEQ)
        spread = sum(r[1] + HEAD * (r[0] - mu) * (r[0] - mu) for r in rows4)
        inverse = 1.0 / jnp.sqrt(spread * (1.0 / WIDTH) + NORM_EPS)
        along = sum(r[2] + (r[0] - mu) * r[3] for r in rows4) * inverse * (1.0 / WIDTH)
        level = sum(r[3] for r in rows4) * (1.0 / WIDTH)
        for i in range(4):
            at = slice(i * HEAD, (i + 1) * HEAD)
            tile = jnp.where(
                sub == 0,
                mu[:, at],
                jnp.where(sub == 1, inverse[:, at], jnp.where(sub == 2, along[:, at], level[:, at])),
            )
            tile = jnp.transpose(tile)
            rows = pl.ds((part * 4 + i) * HEAD, HEAD)
            normed = (attn[rows, :] - tile[:, 0:1]) * tile[:, 1:2]
            normed_head[rows, :] = normed.astype(BF16)
            grad_attn[rows, :] = (
                (gn_head[rows, :].astype(F32) - tile[:, 3:4] - normed * tile[:, 2:3]) * tile[:, 1:2]
            ).astype(BF16)

    def normed_copy(k):
        return remote(
            send_normed.at[k],
            recv_normed.at[back(k)],
            normed_ss.at[k],
            normed_rs.at[back(k)],
            seq_peer(k),
        )

    def pick_normed(k, target):
        low, high = halves(seq_head(k))
        target[k, :HALF] = normed_head[low, :]
        target[k, HALF:] = normed_head[high, :]

    def send_norm(k, carry):
        pick_normed(k, send_normed)
        normed_copy(k).start()
        return carry

    lax.fori_loop(0, 7, send_norm, 0)
    pick_normed(7, recv_normed)

    for i in range(8):
        rows = pl.ds(i * HEAD, HEAD)
        grad_attn_t[:, rows] = jnp.transpose(grad_attn[rows, :])
    for i in range(4):
        rows = pl.ds(i * STEP, STEP)
        for j in range(i + 1):
            cols = pl.ds(j * STEP, STEP)
            ds = dot_t(grad_attn[rows, :], value[cols, :]) * slope[rows, cols]
            slope[rows, cols] = ds
            dscores[rows, cols] = ds.astype(BF16)
        seen = (i + 1) * STEP
        dqkv_head[rows, HEAD : 2 * HEAD] = (
            dot(dscores[rows, :seen], key[:seen, :]) * score_scale
        ).astype(BF16)
    for j in range(4):
        cols = pl.ds(j * STEP, STEP)
        rest = slice(j * STEP, LEN)
        grad_value = dot(grad_attn_t[:, rest], probs[rest, cols])
        grad_key = dot(query_t[:, rest], dscores[rest, cols]) * score_scale
        dqkv_head[cols, 0:HEAD] = jnp.transpose(grad_value).astype(BF16)
        dqkv_head[cols, 2 * HEAD : 3 * HEAD] = jnp.transpose(grad_key).astype(BF16)

    def dqkv_copy(k):
        return remote(
            send_dqkv.at[k], recv_dqkv.at[back(k)], dqkv_ss.at[k], dqkv_rs.at[back(k)], seq_peer(k)
        )

    def pick_dqkv(k, target):
        low, high = halves(seq_head(k))
        target[k, :HALF] = dqkv_head[low, :]
        target[k, HALF:] = dqkv_head[high, :]

    def send_grad(k, carry):
        pick_dqkv(k, send_dqkv)
        dqkv_copy(k).start()
        return carry

    lax.fori_loop(0, 5, send_grad, 0)
    pick_dqkv(5, send_dqkv)
    pick_dqkv(6, send_dqkv)
    pick_dqkv(7, recv_dqkv)

    for k in range(3):
        cot_copy(k).wait_recv()
    pairs = cot_all.reshape(4, 2, ROWS, WIDTH)
    cot_core = remote(pairs.at[:, core], pairs.at[:, core], core_ss, core_rs, core_peer)
    cot_core.start()

    def bucket_sums(i, sums):
        def add_rows(r, sums):
            rows = pl.ds(aligned(i * STEP + r * 8, 8), 8)
            for j in range(2 * (i + 1)):
                cols = pl.ds(j * HEAD, HEAD)
                ds = slope[rows, cols]
                which = bucket[rows, cols]
                sums = tuple(
                    total + jnp.where(which == b, ds, 0.0) for b, total in enumerate(sums)
                )
            return sums

        return lax.fori_loop(0, STEP // 8, add_rows, sums)

    sums = tuple(jnp.zeros((8, HEAD), F32) for _ in range(BUCKETS))
    for i in (0, 3):
        sums = bucket_sums(i, sums)
    dqkv_copy(0).wait_send()
    dqkv_copy(5).start()
    def rows_of_head(j):
        cols = pl.ds(aligned(seq_head(j) * HEAD, HEAD), HEAD)
        normed = recv_normed[j].astype(F32)
        mixed[:, cols] = (normed * gate_rows[:, cols].astype(F32)).astype(BF16)
        gp_gate[:, cols] = (grad_mixed[:, cols] * normed * slope_gate[:, cols]).astype(BF16)

    def take_normed(j, carry):
        normed_copy(back(j)).wait_recv()
        rows_of_head(j)
        return carry

    rows_of_head(7)
    lax.fori_loop(0, 7, take_normed, 0)

    def mixed_block(k):
        return pl.ds(aligned(group_index(k) * HEAD, HEAD), HEAD)

    def mixed_copy(k):
        return remote(
            mixed.at[:, mixed_block(k)],
            mixed_all.at[own_group],
            mixed_ss.at[k],
            mixed_rs.at[6 - k],
            group_peer(k),
        )

    def send_mixed(k, carry):
        mixed_copy(k).start()
        return carry

    lax.fori_loop(0, 7, send_mixed, 0)
    mixed_all[own_group] = mixed[:, mixed_block(7)]
    dqkv_copy(1).wait_send()
    dqkv_copy(6).start()
    for c in range(4):
        cols = pl.ds(c * STEP, STEP)
        layer_out_rows[:, cols] = dot(mixed[...], w_out[:, cols]).astype(BF16)
        ig_acc[:, cols] = dot_t(gp_gate[...], w_gate[cols, :])
    layer_out_copy = pltpu.make_async_copy(layer_out_rows, layer_out_ref.at[0], store_sem.at[0])
    layer_out_copy.start()

    for i in (1, 2):
        sums = bucket_sums(i, sums)
    hist[...] = jnp.zeros((24, HEAD), F32)
    for b in range(BUCKETS):
        hist[b : b + 1, :] = jnp.sum(sums[b], axis=0, keepdims=True)

    def hist_copy(k):
        return remote(hist, hist_recv.at[14 - k], hist_ss.at[k], hist_rs.at[14 - k], dp_peer(k))

    def send_hist(k, carry):
        hist_copy(k).start()
        return carry

    lax.fori_loop(0, 15, send_hist, 0)

    for k in range(7):
        mixed_copy(k).wait_recv()
    cot_core.wait_recv()
    for g in range(8):
        mixed_t[:, g * ROWS : (g + 1) * ROWS] = jnp.transpose(mixed_all[g])
    for c in range(4):
        cols = slice(c * STEP, (c + 1) * STEP)
        product = sum(
            dot(mixed_t[:, q * STEP : (q + 1) * STEP], cot_pair(cot_all, q, cols)) for q in range(4)
        )
        for half in range(2):
            tile = jnp.transpose(product[:, half * HEAD : (half + 1) * HEAD])
            for t in range(SEQ):
                piece[half * SEQ + t, c * 16 : (c + 1) * 16, :] = jnp.concatenate(
                    [tile[t * 8 : t * 8 + 8], tile[HALF + t * 8 : HALF + t * 8 + 8]], axis=0
                ).astype(BF16)

    def piece_copy(k):
        return remote(
            piece.at[piece_index(k)],
            piece_recv.at[14 - k],
            piece_ss.at[k],
            piece_rs.at[14 - k],
            piece_peer(k),
        )

    def send_piece(k, carry):
        piece_copy(k).start()
        return carry

    lax.fori_loop(0, 15, send_piece, 0)

    def add_head(j):
        grad_pre = (recv_dqkv[j].astype(F32) * slope_qkv[j]).astype(BF16)
        for c in range(4):
            cols = pl.ds(c * STEP, STEP)
            ig_acc[:, cols] += dot_t(grad_pre, w_qkv[j, cols, :])

    def take_dqkv(j, carry):
        dqkv_copy(back(j)).wait_recv()
        add_head(j)
        return carry

    add_head(7)
    lax.fori_loop(0, 7, take_dqkv, 0)
    input_grad_rows[...] = ig_acc[...].astype(BF16)
    input_grad_copy = pltpu.make_async_copy(
        input_grad_rows, input_grad_ref.at[0], store_sem.at[1]
    )
    input_grad_copy.start()

    def take_hist(k, total):
        hist_copy(14 - k).wait_recv()
        return total + hist_recv[k]

    hist_sum[...] = lax.fori_loop(0, 15, take_hist, hist[...]) * norm_scale

    def all_copy(k):
        return remote(hist_sum, hist_all.at[back(k)], all_ss.at[k], all_rs.at[back(k)], seq_peer(k))

    def send_all(k, carry):
        all_copy(k).start()
        return carry

    lax.fori_loop(0, 7, send_all, 0)

    def take_piece(k, total):
        piece_copy(14 - k).wait_recv()
        return total + piece_recv[k].astype(F32)

    total = lax.fori_loop(0, 15, take_piece, piece[own_piece].astype(F32)) * norm_scale
    final_send[...] = total.reshape(8, 8, HEAD)

    def final_copy(k):
        return remote(
            final_send.at[group_index(k)],
            final_recv.at[own_group],
            final_ss.at[k],
            final_rs.at[6 - k],
            group_peer(k),
        )

    def send_final(k, carry):
        final_copy(k).start()
        return carry

    lax.fori_loop(0, 7, send_final, 0)
    final_recv[own_group] = final_send[own_group]

    def head_column(j, table):
        column = jnp.sum(hist_all[j], axis=1, keepdims=True)
        return jnp.where(lane[:24] == seq_head(j), column, table)

    hist_all[7] = hist_sum[...]

    def take_all(j, table):
        all_copy(back(j)).wait_recv()
        return head_column(j, table)

    table = head_column(7, jnp.zeros((24, HEAD), F32))
    table = lax.fori_loop(0, 7, take_all, table)
    table = jnp.transpose(jnp.concatenate([table, jnp.zeros((HEAD - 24, HEAD), F32)], axis=0))
    bias_grad_ref[...] = table[:8, :BUCKETS]

    for k in range(7):
        final_copy(k).wait_recv()
    for g in range(8):
        out_grad_ref[:, g * HEAD : (g + 1) * HEAD] = final_recv[g]

    def sent_seq(k, carry):
        for copy in (gn_copy, stat_copy, normed_copy, mixed_copy, all_copy, final_copy):
            copy(k).wait_send()
        return carry

    def sent_many(k, carry):
        piece_copy(k).wait_send()
        hist_copy(k).wait_send()
        return carry

    lax.fori_loop(0, 7, sent_seq, 0)
    lax.fori_loop(0, 15, sent_many, 0)
    for k in range(3):
        cot_copy(k).wait_send()
    cot_core.wait_send()
    for k in range(4, 7):
        qkv_copy(k).wait_send()
    for k in range(2, 7):
        dqkv_copy(k).wait_send()
    layer_out_copy.wait()
    input_grad_copy.wait()


def cot_pair(cot_all, q, cols):
    return jnp.concatenate([cot_all[2 * q, :, cols], cot_all[2 * q + 1, :, cols]], axis=0)


def finish(*refs):
    count = len(refs) // 2
    for source, target in zip(refs[:count], refs[count:]):
        target[...] = source[...]


def body(events, in_weight, out_weight, rab_table, lengths, stamps, cotangent):
    dma = pltpu.SemaphoreType.DMA
    vmem = pltpu.VMEM
    scratch = [
        vmem((SEQ, WIDTH, 3 * HEAD), BF16),
        vmem((WIDTH, WIDTH), BF16),
        vmem((WIDTH, WIDTH), BF16),
        vmem((SEQ, ROWS, 3 * HEAD), F32),
        vmem((ROWS, WIDTH), F32),
        vmem((ROWS, WIDTH), BF16),
        vmem((ROWS, WIDTH), F32),
        vmem((ROWS, WIDTH), BF16),
        vmem((SEQ, ROWS, 3 * HEAD), BF16),
        vmem((SEQ, ROWS, 3 * HEAD), BF16),
        vmem((SEQ, ROWS, HEAD), BF16),
        vmem((LEN, HEAD), BF16),
        vmem((LEN, HEAD), BF16),
        vmem((LEN, HEAD), BF16),
        vmem((LEN, HEAD), BF16),
        vmem((LEN, LEN), F32),
        vmem((LEN, LEN), jnp.int32),
        vmem((LEN, LEN), F32),
        vmem((LEN, LEN), BF16),
        vmem((LEN, LEN), BF16),
        vmem((LEN, HEAD), F32),
        vmem((8, LEN // 2), F32),
        vmem((SEQ, 8, LEN // 2), F32),
        vmem((LEN, HEAD), BF16),
        vmem((LEN, HEAD), BF16),
        vmem((HEAD, LEN), BF16),
        vmem((HEAD, LEN), BF16),
        vmem((SEQ, ROWS, HEAD), BF16),
        vmem((SEQ, ROWS, HEAD), BF16),
        vmem((LEN, 3 * HEAD), BF16),
        vmem((SEQ, ROWS, 3 * HEAD), BF16),
        vmem((SEQ, ROWS, 3 * HEAD), BF16),
        vmem((ROWS, WIDTH), BF16),
        vmem((ROWS, WIDTH), BF16),
        vmem((ROWS, WIDTH), BF16),
        vmem((ROWS, WIDTH), F32),
        vmem((8, ROWS, WIDTH), BF16),
        vmem((8, ROWS, HEAD), BF16),
        vmem((HEAD, 8 * ROWS), BF16),
        vmem((16, HALF, HEAD), BF16),
        vmem((15, HALF, HEAD), BF16),
        vmem((8, 8, HEAD), F32),
        vmem((8, 8, HEAD), F32),
        vmem((24, HEAD), F32),
        vmem((15, 24, HEAD), F32),
        vmem((24, HEAD), F32),
        vmem((SEQ, 24, HEAD), F32),
        pltpu.SMEM((SEQ, BUCKETS), F32),
        pltpu.SMEM((1, 4), jnp.int32),
        vmem((1, LEN), jnp.int32),
        vmem((ROWS, WIDTH), BF16),
        vmem((ROWS, WIDTH), BF16),
        dma((2,)),
        dma((3,)),
        dma((28,)),
        dma((7,)),
        dma((7,)),
        dma((7,)),
        dma((7,)),
        dma((7,)),
        dma((7,)),
        dma((7,)),
        dma((7,)),
        dma((7,)),
        dma((7,)),
        dma((3,)),
        dma((3,)),
        dma,
        dma,
        dma((7,)),
        dma((7,)),
        dma((7,)),
        dma((7,)),
        dma((15,)),
        dma((15,)),
        dma((15,)),
        dma((15,)),
        dma((7,)),
        dma((7,)),
    ]
    hbm = pl.BlockSpec(memory_space=pl.ANY)
    local = pl.BlockSpec(memory_space=pltpu.VMEM)
    shapes = (
        jax.ShapeDtypeStruct((1, ROWS, WIDTH), BF16),
        jax.ShapeDtypeStruct((1, ROWS, WIDTH), BF16),
        jax.ShapeDtypeStruct((8, WIDTH), F32),
        jax.ShapeDtypeStruct((SEQ, BUCKETS), F32),
    )
    results = pl.pallas_call(
        kernel,
        out_shape=shapes,
        in_specs=[hbm] * 7,
        out_specs=(hbm, hbm, local, local),
        scratch_shapes=scratch,
        compiler_params=pltpu.CompilerParams(
            collective_id=0, has_side_effects=True, vmem_limit_bytes=60 * 2**20
        ),
    )(events, in_weight, out_weight, rab_table.T, lengths, stamps, cotangent)
    layer_out, input_grad, out_grad, bias_grad = pl.pallas_call(
        finish,
        out_shape=shapes,
        in_specs=[local] * 4,
        out_specs=(local,) * 4,
    )(*results)
    return (layer_out, input_grad, out_grad.T, bias_grad.T)


def solution(mesh):
    placed = (
        P("dp", "seq", None),
        P(),
        P(),
        P(),
        P("dp", None),
        P("dp", None),
        P("dp", "seq", None),
    )
    return jax.shard_map(
        body,
        mesh=mesh,
        in_specs=placed,
        out_specs=(P("dp", "seq", None), P("dp", "seq", None), P(None, ("dp", "seq")), P()),
        check_vma=False,
    )
```

```python
import functools
import math

import jax
import jax.numpy as jnp
from jax import lax
from jax.experimental import pallas as pl
from jax.experimental.pallas import tpu as pltpu
from jax.sharding import PartitionSpec as P

NORM_EPS = 1e-05
HIDDEN = -1e30
MESH = pl.DeviceIdType.MESH
F32 = jnp.float32
BF16 = jnp.bfloat16

SEQ = 8
ROWS = 128
HALF = 64
LEN = 1024
WIDTH = 1024
HEAD = 128
BUCKETS = 18
STEP = 256


def dot(left, right):
    return jnp.dot(left, right, preferred_element_type=F32)


def dot_t(left, right):
    return lax.dot_general(left, right, (((1,), (1,)), ((), ())), preferred_element_type=F32)


def sigmoid(values):
    return 0.5 * jnp.tanh(0.5 * values) + 0.5


def pick_lane(values, lanes):
    return jnp.take_along_axis(values, lanes, axis=1, mode="promise_in_bounds")


def aligned(value, multiple):
    return pl.multiple_of(value, multiple)


def kernel(
    events_ref,
    in_weight_ref,
    out_weight_ref,
    rab_ref,
    lengths_ref,
    stamps_ref,
    cot_ref,
    layer_out_ref,
    input_grad_ref,
    out_grad_ref,
    bias_grad_ref,
    w_qkv,
    w_gate,
    w_out,
    slope_qkv,
    slope_gate,
    gate_rows,
    grad_mixed,
    gn_rows,
    send_qkv,
    recv_qkv,
    recv_gn,
    query,
    key,
    value,
    gn_head,
    bias,
    bucket,
    slope,
    probs,
    dscores,
    attn,
    stat_send,
    stat_recv,
    centred_head,
    row_stats,
    grad_attn,
    query_t,
    grad_attn_t,
    send_centred,
    recv_centred,
    dqkv_head,
    send_dqkv,
    recv_dqkv,
    event_rows,
    mixed,
    gp_gate,
    ig_acc,
    cot_all,
    mixed_all,
    mixed_t,
    piece,
    piece_recv,
    final_send,
    final_recv,
    hist_recv,
    hist_all,
    rab,
    lengths,
    stamps,
    layer_out_rows,
    input_grad_rows,
    store_sem,
    small_sem,
    load_sem,
    qkv_ss,
    qkv_rs,
    gn_ss,
    gn_rs,
    stat_ss,
    stat_rs,
    centred_ss,
    centred_rs,
    dqkv_ss,
    dqkv_rs,
    cot_ss,
    cot_rs,
    core_ss,
    core_rs,
    mixed_ss,
    mixed_rs,
    final_ss,
    final_rs,
    piece_ss,
    piece_rs,
    hist_ss,
    hist_rs,
    all_ss,
    all_rs,
):
    dp = lax.axis_index("dp")
    seq = lax.axis_index("seq")
    core = lax.rem(dp, 2)
    x_lo = lax.rem(dp // 2, 2)
    y = dp // 4
    score_scale = 1.0 / HEAD**0.5
    norm_scale = 1.0 / math.sqrt(16 * LEN)

    def seq_head(k):
        along_z = lax.rem(seq // 2 + k - 3 * (k // 4), 4)
        return along_z * 2 + lax.rem(seq + k + 1, 2)

    def seq_peer(k):
        return (dp, seq_head(k))

    def back(k):
        upper = k // 4
        return (1 - upper) * lax.rem(8 - k, 4) + upper * (10 - k)

    def y_peer(k):
        return (lax.rem(y + k + 1, 4) * 4 + lax.rem(dp, 4), seq)

    own_group = y * 2 + core

    def group_index(k):
        return lax.rem(own_group + k + 1, 8)

    def group_peer(k):
        other = group_index(k)
        return ((other // 2) * 4 + x_lo * 2 + lax.rem(other, 2), seq)

    own_piece = x_lo * SEQ + seq

    def piece_index(k):
        return lax.rem(own_piece + k + 1, 16)

    def piece_peer(k):
        other = piece_index(k)
        return (y * 4 + (other // SEQ) * 2 + core, lax.rem(other, SEQ))

    core_peer = (dp + 1 - 2 * core, seq)

    def remote(src, dst, ss, rs, device):
        return pltpu.make_async_remote_copy(
            src_ref=src,
            dst_ref=dst,
            send_sem=ss,
            recv_sem=rs,
            device_id=device,
            device_id_type=MESH,
        )

    def wait_bytes(ref, sem):
        pltpu.make_async_copy(ref, ref, sem).wait()

    events_copy = pltpu.make_async_copy(events_ref.at[0], event_rows, load_sem.at[11])
    events_copy.start()

    small_copies = [
        pltpu.make_async_copy(source, target, small_sem.at[n])
        for n, (source, target) in enumerate(
            ((rab_ref, rab), (lengths_ref, lengths), (stamps_ref, stamps))
        )
    ]
    for copy in small_copies:
        copy.start()

    barrier = pltpu.get_barrier_semaphore()

    def greet_piece(k, carry):
        pl.semaphore_signal(barrier, inc=1, device_id=piece_peer(k), device_id_type=MESH)
        return carry

    def greet_group(k, carry):
        pl.semaphore_signal(barrier, inc=1, device_id=group_peer(k), device_id_type=MESH)
        return carry

    lax.fori_loop(0, 15, greet_piece, 0)
    lax.fori_loop(0, 7, greet_group, 0)

    def weight_copy(k, p):
        head = seq_head(k)
        return pltpu.make_async_copy(
            in_weight_ref.at[:, pl.ds(aligned((p + 1) * WIDTH + head * HEAD, HEAD), HEAD)],
            w_qkv.at[k, :, pl.ds(p * HEAD, HEAD)],
            load_sem.at[k],
        )

    for k in range(SEQ):
        for p in range(3):
            weight_copy(k, p).start()
    out_weight_copy = pltpu.make_async_copy(out_weight_ref, w_out, load_sem.at[8])
    out_weight_copy.start()
    gate_copy = pltpu.make_async_copy(
        in_weight_ref.at[:, pl.ds(0, WIDTH)], w_gate, load_sem.at[9]
    )
    gate_copy.start()
    cot_load = pltpu.make_async_copy(cot_ref.at[0], cot_all.at[own_group], load_sem.at[10])
    cot_load.start()

    events_copy.wait()

    def project(k):
        pltpu.make_async_copy(w_qkv.at[k], w_qkv.at[k], load_sem.at[k]).wait()
        pre = dot(event_rows[...], w_qkv[k])
        sig = sigmoid(pre)
        act = pre * sig
        slope_qkv[k] = sig + act * (1.0 - sig)
        return act.astype(BF16)

    def qkv_copy(k):
        return remote(
            send_qkv.at[k], recv_qkv.at[back(k)], qkv_ss.at[k], qkv_rs.at[back(k)], seq_peer(k)
        )

    def project_keep(k, carry):
        send_qkv[k] = project(k)
        return carry

    def project_send(k, carry):
        send_qkv[k] = project(k)
        qkv_copy(k).start()
        return carry

    def send_kept(k, carry):
        qkv_copy(k).start()
        return carry

    lax.fori_loop(0, 1, project_keep, 0)
    pl.semaphore_wait(barrier, 22)
    lax.fori_loop(0, 1, send_kept, 0)
    lax.fori_loop(1, 5, project_send, 0)
    lax.fori_loop(5, 7, project_keep, 0)
    recv_qkv[7] = project(7)
    qkv_copy(0).wait_send()
    qkv_copy(5).start()

    out_weight_copy.wait()
    gate_copy.wait()
    cot_load.wait()
    for c in range(4):
        cols = pl.ds(c * STEP, STEP)
        pre = dot(event_rows[...], w_gate[:, cols])
        sig = sigmoid(pre)
        act = pre * sig
        slope_gate[:, cols] = sig + act * (1.0 - sig)
        gate_b = act.astype(BF16)
        gate_rows[:, cols] = gate_b
        gm = dot_t(cot_all[own_group], w_out[cols, :])
        grad_mixed[:, cols] = gm
        gn_rows[:, cols] = (gm * gate_b.astype(F32)).astype(BF16)

    def gn_copy(k):
        cols = pl.ds(aligned(seq_head(k) * HEAD, HEAD), HEAD)
        return remote(
            gn_rows.at[:, cols], recv_gn.at[back(k)], gn_ss, gn_rs.at[back(k)], seq_peer(k)
        )

    def send_gn(k, carry):
        gn_copy(k).start()
        return carry

    recv_gn[7] = gn_rows[:, pl.ds(aligned(seq * HEAD, HEAD), HEAD)]
    qkv_copy(1).wait_send()
    qkv_copy(6).start()

    def cot_copy(k):
        return remote(
            cot_all.at[own_group], cot_all.at[own_group], cot_ss, cot_rs, y_peer(k)
        )

    def send_cot(k, carry):
        cot_copy(k).start()
        return carry

    lane = lax.broadcasted_iota(jnp.int32, (HEAD, HEAD), 1)
    sub = lax.broadcasted_iota(jnp.int32, (HEAD, HEAD), 0)
    for copy in small_copies:
        copy.wait()
    table_bucket = jnp.minimum(32 - lane[:8], BUCKETS - 1)
    table = jnp.zeros((8, HEAD), F32)
    for b in range(BUCKETS):
        table = jnp.where(table_bucket == b, rab[seq, b], table)
    table = jnp.broadcast_to(table[:1], (HEAD, HEAD))
    end_0 = lengths[0, 0]
    end_1 = end_0 + lengths[0, 1]
    end_2 = end_1 + lengths[0, 2]
    for i in range(8):
        row_stamp = stamps[:, pl.ds(i * HEAD, HEAD)].astype(F32)
        column_stamp = jnp.transpose(jnp.broadcast_to(row_stamp, (HEAD, HEAD))).astype(jnp.int32)
        row_pos = sub + i * HEAD
        first = jnp.where(
            row_pos >= end_2,
            end_2,
            jnp.where(row_pos >= end_1, end_1, jnp.where(row_pos >= end_0, end_0, 0)),
        )
        for j in range(2 * (i // 2) + 2):
            where = (pl.ds(i * HEAD, HEAD), pl.ds(j * HEAD, HEAD))
            key_pos = lane + j * HEAD
            leading = lax.clz(column_stamp - stamps[:, pl.ds(j * HEAD, HEAD)])
            visible = (key_pos >= first) & (key_pos <= row_pos)
            bias[where] = jnp.where(
                visible, pick_lane(table, leading), HIDDEN
            )
            if j <= i:
                bucket[where] = jnp.minimum(32 - leading, BUCKETS - 1)

    def halves(block):
        return (
            pl.ds(aligned(block * HALF, HALF), HALF),
            pl.ds(aligned(LEN - HALF - block * HALF, HALF), HALF),
        )

    def place_qkv(j):
        low, high = halves(seq_head(j))
        for at, rows in ((low, slice(0, HALF)), (high, slice(HALF, ROWS))):
            for p, target in enumerate((value, query, key)):
                target[at, :] = recv_qkv[j, rows, p * HEAD : (p + 1) * HEAD]

    def take_qkv(j, carry):
        qkv_copy(back(j)).wait_recv()
        place_qkv(j)
        return carry

    place_qkv(7)
    qkv_copy(2).wait_send()
    qkv_copy(3).wait_send()
    lax.fori_loop(0, 7, send_gn, 0)
    lax.fori_loop(0, 3, send_cot, 0)
    lax.fori_loop(0, 7, take_qkv, 0)

    def place_gn(j):
        low, high = halves(seq_head(j))
        gn_head[low, :] = recv_gn[j, :HALF]
        gn_head[high, :] = recv_gn[j, HALF:]

    def take_gn(j, carry):
        gn_copy(back(j)).wait_recv()
        place_gn(j)
        return carry

    for i in range(4):
        rows = pl.ds(i * STEP, STEP)
        for j in range(i + 1):
            cols = pl.ds(j * STEP, STEP)
            scores = dot_t(query[rows, :], key[cols, :]) * score_scale + bias[rows, cols]
            sig = sigmoid(scores)
            silu = scores * sig
            probs[rows, cols] = silu.astype(BF16)
            slope[rows, cols] = sig + silu * (1.0 - sig)
        seen = (i + 1) * STEP
        attn[rows, :] = dot(probs[rows, :seen], value[:seen, :])

    place_gn(7)
    lax.fori_loop(0, 7, take_gn, 0)

    def column_stats(i):
        rows = pl.ds(i * HEAD, HEAD)
        a = attn[rows, :]
        g = gn_head[rows, :].astype(F32)
        mean = jnp.mean(a, axis=1, keepdims=True)
        off = a - mean
        centred_head[rows, :] = off.astype(BF16)
        return (
            mean,
            jnp.sum(off * off, axis=1, keepdims=True),
            jnp.sum(g * off, axis=1, keepdims=True),
            jnp.sum(g, axis=1, keepdims=True),
        )

    for i in range(4):
        packed = jnp.zeros((HEAD, HEAD), F32)
        for n, column in enumerate(column_stats(i) + column_stats(i + 4)):
            packed = jnp.where(lane == n, column, packed)
        stat_send[:, pl.ds(i * HEAD, HEAD)] = jnp.transpose(packed)[:8]

    def stat_copy(k):
        return remote(
            stat_send, stat_recv.at[back(k)], stat_ss, stat_rs, seq_peer(k)
        )

    def send_stat(k, carry):
        stat_copy(k).start()
        return carry

    lax.fori_loop(0, 7, send_stat, 0)
    stat_recv[7] = stat_send[...]

    def centred_copy(k):
        return remote(
            send_centred.at[k],
            recv_centred.at[back(k)],
            centred_ss,
            centred_rs.at[back(k)],
            seq_peer(k),
        )

    def pick_centred(k, target):
        low, high = halves(seq_head(k))
        target[k, :HALF] = centred_head[low, :]
        target[k, HALF:] = centred_head[high, :]

    def send_norm(k, carry):
        pick_centred(k, send_centred)
        centred_copy(k).start()
        return carry

    lax.fori_loop(0, 7, send_norm, 0)
    pick_centred(7, recv_centred)

    for i in range(8):
        rows = pl.ds(i * HEAD, HEAD)
        query_t[:, rows] = jnp.transpose(query[rows, :])

    wait_bytes(stat_recv.at[:7], stat_rs)

    wait_bytes(cot_all.at[:3], cot_rs)
    pairs = cot_all.reshape(4, 2, ROWS, WIDTH)
    cot_core = remote(pairs.at[:, core], pairs.at[:, core], core_ss, core_rs, core_peer)
    cot_core.start()

    for part in range(2):
        rows4 = [[stat_recv[j, part * 4 + n : part * 4 + n + 1, :] for n in range(4)] for j in range(SEQ)]
        mu = sum(r[0] for r in rows4) * (1.0 / SEQ)
        spread = sum(r[1] + HEAD * (r[0] - mu) * (r[0] - mu) for r in rows4)
        inverse = 1.0 / jnp.sqrt(spread * (1.0 / WIDTH) + NORM_EPS)
        along = sum(r[2] + (r[0] - mu) * r[3] for r in rows4) * inverse * (1.0 / WIDTH)
        level = sum(r[3] for r in rows4) * (1.0 / WIDTH)
        columns = jnp.concatenate(
            [mu, inverse, along, level] + [r[0] - mu for r in rows4] + [jnp.zeros_like(mu)] * 4, axis=0
        )
        for i in range(4):
            at = slice(i * HEAD, (i + 1) * HEAD)
            tile = jnp.transpose(
                jnp.concatenate([columns[:, at], jnp.zeros((HEAD - 16, HEAD), F32)], axis=0)
            )
            row_stats[pl.ds((part * 4 + i) * HEAD, HEAD), :] = tile

    for i in range(8):
        rows = pl.ds(i * HEAD, HEAD)
        tile = row_stats[rows, :]
        normed = (attn[rows, :] - tile[:, 0:1]) * tile[:, 1:2]
        grad_attn[rows, :] = (
            (gn_head[rows, :].astype(F32) - tile[:, 3:4] - normed * tile[:, 2:3]) * tile[:, 1:2]
        ).astype(BF16)

    for i in range(8):
        rows = pl.ds(i * HEAD, HEAD)
        grad_attn_t[:, rows] = jnp.transpose(grad_attn[rows, :])
    for i in range(4):
        rows = pl.ds(i * STEP, STEP)
        for j in range(i + 1):
            cols = pl.ds(j * STEP, STEP)
            ds = dot_t(grad_attn[rows, :], value[cols, :]) * slope[rows, cols]
            slope[rows, cols] = ds
            dscores[rows, cols] = ds.astype(BF16)
        seen = (i + 1) * STEP
        dqkv_head[rows, HEAD : 2 * HEAD] = (
            dot(dscores[rows, :seen], key[:seen, :]) * score_scale
        ).astype(BF16)
    for j in range(4):
        cols = pl.ds(j * STEP, STEP)
        rest = slice(j * STEP, LEN)
        grad_value = dot(grad_attn_t[:, rest], probs[rest, cols])
        grad_key = dot(query_t[:, rest], dscores[rest, cols]) * score_scale
        dqkv_head[cols, 0:HEAD] = jnp.transpose(grad_value).astype(BF16)
        dqkv_head[cols, 2 * HEAD : 3 * HEAD] = jnp.transpose(grad_key).astype(BF16)

    def dqkv_copy(k):
        return remote(
            send_dqkv.at[k], recv_dqkv.at[back(k)], dqkv_ss, dqkv_rs.at[back(k)], seq_peer(k)
        )

    def pick_dqkv(k, target):
        low, high = halves(seq_head(k))
        target[k, :HALF] = dqkv_head[low, :]
        target[k, HALF:] = dqkv_head[high, :]

    def send_grad(k, carry):
        pick_dqkv(k, send_dqkv)
        dqkv_copy(k).start()
        return carry

    lax.fori_loop(0, 7, send_grad, 0)
    pick_dqkv(7, recv_dqkv)

    low, high = halves(seq)
    own_stats = jnp.concatenate([row_stats[low, :], row_stats[high, :]], axis=0)
    for j in (7, 0, 1, 2, 3, 4, 5, 6):
        if j < 7:
            centred_copy(back(j)).wait_recv()
        cols = pl.ds(aligned(seq_head(j) * HEAD, HEAD), HEAD)
        normed = (recv_centred[j].astype(F32) + own_stats[:, 4 + j : 5 + j]) * own_stats[:, 1:2]
        mixed[:, cols] = (normed * gate_rows[:, cols].astype(F32)).astype(BF16)
        gp_gate[:, cols] = (grad_mixed[:, cols] * normed * slope_gate[:, cols]).astype(BF16)

    def mixed_block(k):
        return pl.ds(aligned(group_index(k) * HEAD, HEAD), HEAD)

    def mixed_copy(k):
        return remote(
            mixed.at[:, mixed_block(k)],
            mixed_all.at[own_group],
            mixed_ss,
            mixed_rs,
            group_peer(k),
        )

    def send_mixed(k, carry):
        mixed_copy(k).start()
        return carry

    lax.fori_loop(0, 7, send_mixed, 0)
    mixed_all[own_group] = mixed[:, mixed_block(7)]
    def bucket_sums(i, sums):
        def add_rows(r, sums):
            for block in (i, 7 - i):
                rows = pl.ds(aligned(block * HEAD + r * 8, 8), 8)
                for j in range(block + 1):
                    cols = pl.ds(j * HEAD, HEAD)
                    ds = slope[rows, cols]
                    which = bucket[rows, cols]
                    sums = tuple(
                        total + jnp.where(which == b, ds, 0.0) for b, total in enumerate(sums)
                    )
            return sums

        return lax.fori_loop(0, HEAD // 8, add_rows, sums)

    sums = tuple(jnp.zeros((8, HEAD), F32) for _ in range(BUCKETS))
    for i in range(4):
        sums = bucket_sums(i, sums)
    sums = [jnp.sum(total, axis=0, keepdims=True) for total in sums]
    sums = jnp.transpose(
        jnp.concatenate(sums + [jnp.zeros((HEAD - BUCKETS, HEAD), F32)], axis=0)
    )
    hist_recv[own_piece] = jnp.sum(sums.reshape(HEAD // 8, 8, HEAD), axis=0)

    def hist_copy(k):
        return remote(
            hist_recv.at[own_piece], hist_recv.at[own_piece], hist_ss, hist_rs, piece_peer(k)
        )

    def send_hist(k, carry):
        hist_copy(k).start()
        return carry

    lax.fori_loop(0, 15, send_hist, 0)

    for c in range(4):
        cols = pl.ds(c * STEP, STEP)
        layer_out_rows[:, cols] = dot(mixed[...], w_out[:, cols]).astype(BF16)
        ig_acc[:, cols] = dot_t(gp_gate[...], w_gate[cols, :])
    layer_out_copy = pltpu.make_async_copy(layer_out_rows, layer_out_ref.at[0], store_sem.at[0])
    layer_out_copy.start()

    wait_bytes(mixed_all.at[:7], mixed_rs)
    cot_core.wait_recv()
    for g in range(8):
        mixed_t[:, g * ROWS : (g + 1) * ROWS] = jnp.transpose(mixed_all[g])
    for c in range(4):
        cols = slice(c * STEP, (c + 1) * STEP)
        product = sum(
            dot(mixed_t[:, q * STEP : (q + 1) * STEP], cot_pair(cot_all, q, cols)) for q in range(4)
        )
        for half in range(2):
            tile = jnp.transpose(product[:, half * HEAD : (half + 1) * HEAD])
            for t in range(SEQ):
                piece[half * SEQ + t, c * 16 : (c + 1) * 16, :] = jnp.concatenate(
                    [tile[t * 8 : t * 8 + 8], tile[HALF + t * 8 : HALF + t * 8 + 8]], axis=0
                ).astype(BF16)

    def piece_copy(k):
        return remote(
            piece.at[piece_index(k)],
            piece_recv.at[14 - k],
            piece_ss,
            piece_rs,
            piece_peer(k),
        )

    def send_piece(k, carry):
        piece_copy(k).start()
        return carry

    lax.fori_loop(0, 15, send_piece, 0)

    def add_head(j):
        grad_pre = (recv_dqkv[j].astype(F32) * slope_qkv[j]).astype(BF16)
        for c in range(4):
            cols = pl.ds(c * STEP, STEP)
            ig_acc[:, cols] += dot_t(grad_pre, w_qkv[j, cols, :])

    def take_dqkv(j, carry):
        dqkv_copy(back(j)).wait_recv()
        add_head(j)
        return carry

    add_head(7)
    lax.fori_loop(0, 4, take_dqkv, 0)
    wait_bytes(hist_recv.at[:15], hist_rs)
    heads = jnp.sum(hist_recv[:SEQ] + hist_recv[SEQ:], axis=1) * norm_scale
    hist_all[own_group] = heads

    def all_copy(k):
        return remote(
            hist_all.at[own_group], hist_all.at[own_group], all_ss, all_rs, group_peer(k)
        )

    def send_all(k, carry):
        all_copy(k).start()
        return carry

    lax.fori_loop(0, 7, send_all, 0)

    def take_piece(k, total):
        return total + piece_recv[k].astype(F32)

    wait_bytes(piece_recv, piece_rs)
    total = lax.fori_loop(0, 15, take_piece, piece[own_piece].astype(F32)) * norm_scale
    final_send[...] = total.reshape(8, 8, HEAD)

    def final_copy(k):
        return remote(
            final_send.at[group_index(k)],
            final_recv.at[own_group],
            final_ss,
            final_rs,
            group_peer(k),
        )

    def send_final(k, carry):
        final_copy(k).start()
        return carry

    lax.fori_loop(0, 7, send_final, 0)
    final_recv[own_group] = final_send[own_group]

    lax.fori_loop(4, 7, take_dqkv, 0)
    input_grad_rows[...] = ig_acc[...].astype(BF16)
    input_grad_copy = pltpu.make_async_copy(
        input_grad_rows, input_grad_ref.at[0], store_sem.at[1]
    )
    input_grad_copy.start()

    wait_bytes(hist_all.at[:7], all_rs)
    bias_grad_ref[...] = jnp.sum(hist_all[...], axis=0)[:, :BUCKETS]

    wait_bytes(final_recv.at[:7], final_rs)
    for g in range(8):
        out_grad_ref[:, g * HEAD : (g + 1) * HEAD] = final_recv[g]

    wait_bytes(recv_gn.at[:7], gn_ss)
    wait_bytes(stat_recv.at[:7], stat_ss)
    wait_bytes(recv_centred.at[:7], centred_ss)
    wait_bytes(mixed_all.at[:7], mixed_ss)
    wait_bytes(hist_all.at[:7], all_ss)
    wait_bytes(final_recv.at[:7], final_ss)
    wait_bytes(piece_recv, piece_ss)
    wait_bytes(hist_recv.at[:15], hist_ss)
    wait_bytes(cot_all.at[:3], cot_ss)
    cot_core.wait_send()
    for k in range(4, 7):
        qkv_copy(k).wait_send()
    wait_bytes(recv_dqkv.at[:7], dqkv_ss)
    layer_out_copy.wait()
    input_grad_copy.wait()


def cot_pair(cot_all, q, cols):
    return jnp.concatenate([cot_all[2 * q, :, cols], cot_all[2 * q + 1, :, cols]], axis=0)


def finish(*refs):
    count = len(refs) // 2
    for source, target in zip(refs[:count], refs[count:]):
        target[...] = source[...]


def body(events, in_weight, out_weight, rab_table, lengths, stamps, cotangent):
    dma = pltpu.SemaphoreType.DMA
    vmem = pltpu.VMEM
    scratch = [
        vmem((SEQ, WIDTH, 3 * HEAD), BF16),
        vmem((WIDTH, WIDTH), BF16),
        vmem((WIDTH, WIDTH), BF16),
        vmem((SEQ, ROWS, 3 * HEAD), F32),
        vmem((ROWS, WIDTH), F32),
        vmem((ROWS, WIDTH), BF16),
        vmem((ROWS, WIDTH), F32),
        vmem((ROWS, WIDTH), BF16),
        vmem((SEQ, ROWS, 3 * HEAD), BF16),
        vmem((SEQ, ROWS, 3 * HEAD), BF16),
        vmem((SEQ, ROWS, HEAD), BF16),
        vmem((LEN, HEAD), BF16),
        vmem((LEN, HEAD), BF16),
        vmem((LEN, HEAD), BF16),
        vmem((LEN, HEAD), BF16),
        vmem((LEN, LEN), F32),
        vmem((LEN, LEN), jnp.int32),
        vmem((LEN, LEN), F32),
        vmem((LEN, LEN), BF16),
        vmem((LEN, LEN), BF16),
        vmem((LEN, HEAD), F32),
        vmem((8, LEN // 2), F32),
        vmem((SEQ, 8, LEN // 2), F32),
        vmem((LEN, HEAD), BF16),
        vmem((LEN, HEAD), F32),
        vmem((LEN, HEAD), BF16),
        vmem((HEAD, LEN), BF16),
        vmem((HEAD, LEN), BF16),
        vmem((SEQ, ROWS, HEAD), BF16),
        vmem((SEQ, ROWS, HEAD), BF16),
        vmem((LEN, 3 * HEAD), BF16),
        vmem((SEQ, ROWS, 3 * HEAD), BF16),
        vmem((SEQ, ROWS, 3 * HEAD), BF16),
        vmem((ROWS, WIDTH), BF16),
        vmem((ROWS, WIDTH), BF16),
        vmem((ROWS, WIDTH), BF16),
        vmem((ROWS, WIDTH), F32),
        vmem((8, ROWS, WIDTH), BF16),
        vmem((8, ROWS, HEAD), BF16),
        vmem((HEAD, 8 * ROWS), BF16),
        vmem((16, HALF, HEAD), BF16),
        vmem((15, HALF, HEAD), BF16),
        vmem((8, 8, HEAD), F32),
        vmem((8, 8, HEAD), F32),
        vmem((16, 8, HEAD), F32),
        vmem((8, 8, HEAD), F32),
        pltpu.SMEM((SEQ, BUCKETS), F32),
        pltpu.SMEM((1, 4), jnp.int32),
        vmem((1, LEN), jnp.int32),
        vmem((ROWS, WIDTH), BF16),
        vmem((ROWS, WIDTH), BF16),
        dma((2,)),
        dma((3,)),
        dma((12,)),
        dma((7,)),
        dma((7,)),
        dma,
        dma((7,)),
        dma,
        dma,
        dma,
        dma((7,)),
        dma,
        dma((7,)),
        dma,
        dma,
        dma,
        dma,
        dma,
        dma,
        dma,
        dma,
        dma,
        dma,
        dma,
        dma,
        dma,
        dma,
    ]
    hbm = pl.BlockSpec(memory_space=pl.ANY)
    local = pl.BlockSpec(memory_space=pltpu.VMEM)
    shapes = (
        jax.ShapeDtypeStruct((1, ROWS, WIDTH), BF16),
        jax.ShapeDtypeStruct((1, ROWS, WIDTH), BF16),
        jax.ShapeDtypeStruct((8, WIDTH), F32),
        jax.ShapeDtypeStruct((SEQ, BUCKETS), F32),
    )
    results = pl.pallas_call(
        kernel,
        out_shape=shapes,
        in_specs=[hbm] * 7,
        out_specs=(hbm, hbm, local, local),
        scratch_shapes=scratch,
        compiler_params=pltpu.CompilerParams(
            collective_id=0, has_side_effects=True, vmem_limit_bytes=60 * 2**20
        ),
    )(events, in_weight, out_weight, rab_table.T, lengths, stamps, cotangent)
    layer_out, input_grad, out_grad, bias_grad = pl.pallas_call(
        finish,
        out_shape=shapes,
        in_specs=[local] * 4,
        out_specs=(local,) * 4,
    )(*results)
    return (layer_out, input_grad, out_grad.T, bias_grad.T)


def solution(mesh):
    placed = (
        P("dp", "seq", None),
        P(),
        P(),
        P(),
        P("dp", None),
        P("dp", None),
        P("dp", "seq", None),
    )
    return jax.shard_map(
        body,
        mesh=mesh,
        in_specs=placed,
        out_specs=(P("dp", "seq", None), P("dp", "seq", None), P(None, ("dp", "seq")), P()),
        check_vma=False,
    )
```

```python
import functools
import math

import jax
import jax.numpy as jnp
from jax import lax
from jax.experimental import pallas as pl
from jax.experimental.pallas import tpu as pltpu
from jax.sharding import PartitionSpec as P

NORM_EPS = 1e-05
HIDDEN = -1e30
MESH = pl.DeviceIdType.MESH
F32 = jnp.float32
BF16 = jnp.bfloat16

SEQ = 8
ROWS = 128
HALF = 64
LEN = 1024
WIDTH = 1024
HEAD = 128
BUCKETS = 18
STEP = 256
PACKS = 3


def dot(left, right):
    return jnp.dot(left, right, preferred_element_type=F32)


def dot_t(left, right):
    return lax.dot_general(left, right, (((1,), (1,)), ((), ())), preferred_element_type=F32)


def sigmoid(values):
    return 0.5 * jnp.tanh(0.5 * values) + 0.5


def pack_groups(p):
    return [(a, 7 * p + a) for a in range(7) if 7 * p + a < 16]


def pick_lane(values, lanes):
    return jnp.take_along_axis(values, lanes, axis=1, mode="promise_in_bounds")


def aligned(value, multiple):
    return pl.multiple_of(value, multiple)


def kernel(
    events_ref,
    in_weight_ref,
    out_weight_ref,
    rab_ref,
    lengths_ref,
    stamps_ref,
    cot_ref,
    layer_out_ref,
    input_grad_ref,
    out_grad_ref,
    bias_grad_ref,
    w_qkv,
    w_gate,
    w_out,
    slope_qkv,
    slope_gate,
    gate_rows,
    grad_mixed,
    gn_rows,
    send_qkv,
    recv_qkv,
    recv_gn,
    query,
    key,
    value,
    gn_head,
    bias,
    limit,
    last_key,
    slope,
    probs,
    dscores,
    attn,
    stat_send,
    stat_recv,
    centred_head,
    row_stats,
    grad_attn,
    query_t,
    grad_attn_t,
    send_centred,
    recv_centred,
    dqkv_head,
    send_dqkv,
    recv_dqkv,
    event_rows,
    mixed,
    gp_gate,
    ig_acc,
    cot_all,
    mixed_all,
    mixed_t,
    piece,
    piece_recv,
    final_send,
    final_recv,
    hist_recv,
    hist_all,
    rab,
    lengths,
    stamps,
    layer_out_rows,
    input_grad_rows,
    store_sem,
    small_sem,
    load_sem,
    qkv_ss,
    qkv_rs,
    gn_ss,
    gn_rs,
    stat_ss,
    stat_rs,
    centred_ss,
    centred_rs,
    dqkv_ss,
    dqkv_rs,
    cot_ss,
    cot_rs,
    core_ss,
    core_rs,
    mixed_ss,
    mixed_rs,
    final_ss,
    final_rs,
    piece_ss,
    piece_rs,
    hist_ss,
    hist_rs,
    all_ss,
    all_rs,
):
    dp = lax.axis_index("dp")
    seq = lax.axis_index("seq")
    core = lax.rem(dp, 2)
    x_lo = lax.rem(dp // 2, 2)
    y = dp // 4
    score_scale = 1.0 / HEAD**0.5
    norm_scale = 1.0 / math.sqrt(16 * LEN)

    def seq_head(k):
        along_z = lax.rem(seq // 2 + k - 3 * (k // 4), 4)
        return along_z * 2 + lax.rem(seq + k + 1, 2)

    def seq_peer(k):
        return (dp, seq_head(k))

    def back(k):
        upper = k // 4
        return (1 - upper) * lax.rem(8 - k, 4) + upper * (10 - k)

    def y_peer(k):
        return (lax.rem(y + k + 1, 4) * 4 + lax.rem(dp, 4), seq)

    own_group = y * 2 + core

    def group_index(k):
        return lax.rem(own_group + k + 1, 8)

    def group_peer(k):
        other = group_index(k)
        return ((other // 2) * 4 + x_lo * 2 + lax.rem(other, 2), seq)

    own_piece = x_lo * SEQ + seq

    def piece_index(k):
        return lax.rem(own_piece + k + 1, 16)

    def piece_peer(k):
        other = piece_index(k)
        return (y * 4 + (other // SEQ) * 2 + core, lax.rem(other, SEQ))

    core_peer = (dp + 1 - 2 * core, seq)

    def remote(src, dst, ss, rs, device):
        return pltpu.make_async_remote_copy(
            src_ref=src,
            dst_ref=dst,
            send_sem=ss,
            recv_sem=rs,
            device_id=device,
            device_id_type=MESH,
        )

    def wait_bytes(ref, sem):
        pltpu.make_async_copy(ref, ref, sem).wait()

    events_copy = pltpu.make_async_copy(events_ref.at[0], event_rows, load_sem.at[11])
    events_copy.start()

    small_copies = [
        pltpu.make_async_copy(source, target, small_sem.at[n])
        for n, (source, target) in enumerate(
            ((rab_ref, rab), (lengths_ref, lengths), (stamps_ref, stamps))
        )
    ]
    for copy in small_copies:
        copy.start()

    barrier = pltpu.get_barrier_semaphore()

    def greet_piece(k, carry):
        pl.semaphore_signal(barrier, inc=1, device_id=piece_peer(k), device_id_type=MESH)
        return carry

    def greet_group(k, carry):
        pl.semaphore_signal(barrier, inc=1, device_id=group_peer(k), device_id_type=MESH)
        return carry

    lax.fori_loop(0, 15, greet_piece, 0)
    lax.fori_loop(0, 7, greet_group, 0)

    def weight_copy(k, p):
        head = seq_head(k)
        return pltpu.make_async_copy(
            in_weight_ref.at[:, pl.ds(aligned((p + 1) * WIDTH + head * HEAD, HEAD), HEAD)],
            w_qkv.at[k, :, pl.ds(p * HEAD, HEAD)],
            load_sem.at[k],
        )

    for k in range(SEQ):
        for p in range(3):
            weight_copy(k, p).start()
    out_weight_copy = pltpu.make_async_copy(out_weight_ref, w_out, load_sem.at[8])
    out_weight_copy.start()
    gate_copy = pltpu.make_async_copy(
        in_weight_ref.at[:, pl.ds(0, WIDTH)], w_gate, load_sem.at[9]
    )
    gate_copy.start()
    cot_load = pltpu.make_async_copy(cot_ref.at[0], cot_all.at[own_group], load_sem.at[10])
    cot_load.start()

    events_copy.wait()

    def project(k):
        pltpu.make_async_copy(w_qkv.at[k], w_qkv.at[k], load_sem.at[k]).wait()
        pre = dot(event_rows[...], w_qkv[k])
        sig = sigmoid(pre)
        act = pre * sig
        slope_qkv[k] = sig + act * (1.0 - sig)
        return act.astype(BF16)

    def qkv_copy(k):
        return remote(
            send_qkv.at[k], recv_qkv.at[back(k)], qkv_ss.at[k], qkv_rs.at[back(k)], seq_peer(k)
        )

    def project_keep(k, carry):
        send_qkv[k] = project(k)
        return carry

    def project_send(k, carry):
        send_qkv[k] = project(k)
        qkv_copy(k).start()
        return carry

    def send_kept(k, carry):
        qkv_copy(k).start()
        return carry

    lax.fori_loop(0, 1, project_keep, 0)
    pl.semaphore_wait(barrier, 22)
    lax.fori_loop(0, 1, send_kept, 0)
    lax.fori_loop(1, 5, project_send, 0)
    lax.fori_loop(5, 7, project_keep, 0)
    recv_qkv[7] = project(7)
    qkv_copy(0).wait_send()
    qkv_copy(5).start()

    out_weight_copy.wait()
    gate_copy.wait()
    cot_load.wait()
    for c in range(4):
        cols = pl.ds(c * STEP, STEP)
        pre = dot(event_rows[...], w_gate[:, cols])
        sig = sigmoid(pre)
        act = pre * sig
        slope_gate[:, cols] = sig + act * (1.0 - sig)
        gate_b = act.astype(BF16)
        gate_rows[:, cols] = gate_b
        gm = dot_t(cot_all[own_group], w_out[cols, :])
        grad_mixed[:, cols] = gm
        gn_rows[:, cols] = (gm * gate_b.astype(F32)).astype(BF16)

    def gn_copy(k):
        cols = pl.ds(aligned(seq_head(k) * HEAD, HEAD), HEAD)
        return remote(
            gn_rows.at[:, cols], recv_gn.at[back(k)], gn_ss, gn_rs.at[back(k)], seq_peer(k)
        )

    def send_gn(k, carry):
        gn_copy(k).start()
        return carry

    recv_gn[7] = gn_rows[:, pl.ds(aligned(seq * HEAD, HEAD), HEAD)]
    qkv_copy(1).wait_send()
    qkv_copy(6).start()

    def cot_copy(k):
        return remote(
            cot_all.at[own_group], cot_all.at[own_group], cot_ss, cot_rs, y_peer(k)
        )

    def send_cot(k, carry):
        cot_copy(k).start()
        return carry

    lane = lax.broadcasted_iota(jnp.int32, (HEAD, HEAD), 1)
    sub = lax.broadcasted_iota(jnp.int32, (HEAD, HEAD), 0)
    for copy in small_copies:
        copy.wait()
    table_bucket = jnp.minimum(32 - lane[:8], BUCKETS - 1)
    table = jnp.zeros((8, HEAD), F32)
    for b in range(BUCKETS):
        table = jnp.where(table_bucket == b, rab[seq, b], table)
    table = jnp.broadcast_to(table[:1], (HEAD, HEAD))
    group = sum((lane[:8] >= BUCKETS * a).astype(jnp.int32) for a in range(1, 8))
    which = lane - BUCKETS * sum((lane >= BUCKETS * a).astype(jnp.int32) for a in range(1, 8))
    power = jnp.left_shift(1, jnp.minimum(which, BUCKETS - 2))
    end_0 = lengths[0, 0]
    end_1 = end_0 + lengths[0, 1]
    end_2 = end_1 + lengths[0, 2]
    for i in range(8):
        row_stamp = stamps[:, pl.ds(i * HEAD, HEAD)].astype(F32)
        column_stamp = jnp.transpose(jnp.broadcast_to(row_stamp, (HEAD, HEAD))).astype(jnp.int32)
        limits = jnp.where(which < BUCKETS - 1, column_stamp - power, 1 << 30)
        for p in range(PACKS):
            packed = jnp.full((8, HEAD), -1, jnp.int32)
            for a, g in pack_groups(p):
                packed = jnp.where(group == a, limits[g * 8 : g * 8 + 8], packed)
            limit[i, p * 8 : p * 8 + 8, :] = packed
        row_pos = sub + i * HEAD
        first = jnp.where(
            row_pos >= end_2,
            end_2,
            jnp.where(row_pos >= end_1, end_1, jnp.where(row_pos >= end_0, end_0, 0)),
        )
        for j in range(2 * (i // 2) + 2):
            where = (pl.ds(i * HEAD, HEAD), pl.ds(j * HEAD, HEAD))
            key_pos = lane + j * HEAD
            leading = lax.clz(column_stamp - stamps[:, pl.ds(j * HEAD, HEAD)])
            visible = (key_pos >= first) & (key_pos <= row_pos)
            bias[where] = jnp.where(
                visible, pick_lane(table, leading), HIDDEN
            )

    def find_last(i):
        keys = jnp.concatenate(
            [
                jnp.broadcast_to(stamps[:, j * HEAD : (j + 1) * HEAD], (8 * PACKS, HEAD))
                for j in range(i + 1)
            ],
            axis=0,
        )
        most = jnp.concatenate([limit[i]] * (i + 1), axis=0)
        last = jnp.full(most.shape, -1, jnp.int32)
        for step in (64, 32, 16, 8, 4, 2, 1, 1):
            later = last + step
            last = jnp.where(pick_lane(keys, later) <= most, later, last)
        last_key[i, : 8 * PACKS * (i + 1), :] = last

    def halves(block):
        return (
            pl.ds(aligned(block * HALF, HALF), HALF),
            pl.ds(aligned(LEN - HALF - block * HALF, HALF), HALF),
        )

    def place_qkv(j):
        low, high = halves(seq_head(j))
        for at, rows in ((low, slice(0, HALF)), (high, slice(HALF, ROWS))):
            for p, target in enumerate((value, query, key)):
                target[at, :] = recv_qkv[j, rows, p * HEAD : (p + 1) * HEAD]

    def take_qkv(j, carry):
        qkv_copy(back(j)).wait_recv()
        place_qkv(j)
        return carry

    place_qkv(7)
    qkv_copy(2).wait_send()
    qkv_copy(3).wait_send()
    lax.fori_loop(0, 7, send_gn, 0)
    lax.fori_loop(0, 3, send_cot, 0)
    for i in range(8):
        find_last(i)
    lax.fori_loop(0, 7, take_qkv, 0)

    def place_gn(j):
        low, high = halves(seq_head(j))
        gn_head[low, :] = recv_gn[j, :HALF]
        gn_head[high, :] = recv_gn[j, HALF:]

    def take_gn(j, carry):
        gn_copy(back(j)).wait_recv()
        place_gn(j)
        return carry

    for i in range(4):
        rows = pl.ds(i * STEP, STEP)
        for j in range(i + 1):
            cols = pl.ds(j * STEP, STEP)
            scores = dot_t(query[rows, :], key[cols, :]) * score_scale + bias[rows, cols]
            sig = sigmoid(scores)
            silu = scores * sig
            probs[rows, cols] = silu.astype(BF16)
            slope[rows, cols] = sig + silu * (1.0 - sig)
        seen = (i + 1) * STEP
        attn[rows, :] = dot(probs[rows, :seen], value[:seen, :])

    place_gn(7)
    lax.fori_loop(0, 7, take_gn, 0)

    def column_stats(i):
        rows = pl.ds(i * HEAD, HEAD)
        a = attn[rows, :]
        g = gn_head[rows, :].astype(F32)
        mean = jnp.mean(a, axis=1, keepdims=True)
        off = a - mean
        centred_head[rows, :] = off.astype(BF16)
        return (
            mean,
            jnp.sum(off * off, axis=1, keepdims=True),
            jnp.sum(g * off, axis=1, keepdims=True),
            jnp.sum(g, axis=1, keepdims=True),
        )

    for i in range(4):
        packed = jnp.zeros((HEAD, HEAD), F32)
        for n, column in enumerate(column_stats(i) + column_stats(i + 4)):
            packed = jnp.where(lane == n, column, packed)
        stat_send[:, pl.ds(i * HEAD, HEAD)] = jnp.transpose(packed)[:8]

    def stat_copy(k):
        return remote(
            stat_send, stat_recv.at[back(k)], stat_ss, stat_rs, seq_peer(k)
        )

    def send_stat(k, carry):
        stat_copy(k).start()
        return carry

    lax.fori_loop(0, 7, send_stat, 0)
    stat_recv[7] = stat_send[...]

    def centred_copy(k):
        return remote(
            send_centred.at[k],
            recv_centred.at[back(k)],
            centred_ss,
            centred_rs.at[back(k)],
            seq_peer(k),
        )

    def pick_centred(k, target):
        low, high = halves(seq_head(k))
        target[k, :HALF] = centred_head[low, :]
        target[k, HALF:] = centred_head[high, :]

    def send_norm(k, carry):
        pick_centred(k, send_centred)
        centred_copy(k).start()
        return carry

    lax.fori_loop(0, 7, send_norm, 0)
    pick_centred(7, recv_centred)

    for i in range(8):
        rows = pl.ds(i * HEAD, HEAD)
        query_t[:, rows] = jnp.transpose(query[rows, :])

    wait_bytes(stat_recv.at[:7], stat_rs)

    wait_bytes(cot_all.at[:3], cot_rs)
    pairs = cot_all.reshape(4, 2, ROWS, WIDTH)
    cot_core = remote(pairs.at[:, core], pairs.at[:, core], core_ss, core_rs, core_peer)
    cot_core.start()

    for part in range(2):
        rows4 = [[stat_recv[j, part * 4 + n : part * 4 + n + 1, :] for n in range(4)] for j in range(SEQ)]
        mu = sum(r[0] for r in rows4) * (1.0 / SEQ)
        spread = sum(r[1] + HEAD * (r[0] - mu) * (r[0] - mu) for r in rows4)
        inverse = 1.0 / jnp.sqrt(spread * (1.0 / WIDTH) + NORM_EPS)
        along = sum(r[2] + (r[0] - mu) * r[3] for r in rows4) * inverse * (1.0 / WIDTH)
        level = sum(r[3] for r in rows4) * (1.0 / WIDTH)
        columns = jnp.concatenate(
            [mu, inverse, along, level] + [r[0] - mu for r in rows4] + [jnp.zeros_like(mu)] * 4, axis=0
        )
        for i in range(4):
            at = slice(i * HEAD, (i + 1) * HEAD)
            tile = jnp.transpose(
                jnp.concatenate([columns[:, at], jnp.zeros((HEAD - 16, HEAD), F32)], axis=0)
            )
            row_stats[pl.ds((part * 4 + i) * HEAD, HEAD), :] = tile

    for i in range(8):
        rows = pl.ds(i * HEAD, HEAD)
        tile = row_stats[rows, :]
        normed = (attn[rows, :] - tile[:, 0:1]) * tile[:, 1:2]
        grad_attn[rows, :] = (
            (gn_head[rows, :].astype(F32) - tile[:, 3:4] - normed * tile[:, 2:3]) * tile[:, 1:2]
        ).astype(BF16)

    for i in range(8):
        rows = pl.ds(i * HEAD, HEAD)
        grad_attn_t[:, rows] = jnp.transpose(grad_attn[rows, :])
    for i in range(4):
        rows = pl.ds(i * STEP, STEP)
        for j in range(i + 1):
            cols = pl.ds(j * STEP, STEP)
            ds = dot_t(grad_attn[rows, :], value[cols, :]) * slope[rows, cols]
            dscores[rows, cols] = ds.astype(BF16)
        seen = (i + 1) * STEP
        dqkv_head[rows, HEAD : 2 * HEAD] = (
            dot(dscores[rows, :seen], key[:seen, :]) * score_scale
        ).astype(BF16)
    for j in range(4):
        cols = pl.ds(j * STEP, STEP)
        rest = slice(j * STEP, LEN)
        grad_value = dot(grad_attn_t[:, rest], probs[rest, cols])
        grad_key = dot(query_t[:, rest], dscores[rest, cols]) * score_scale
        dqkv_head[cols, 0:HEAD] = jnp.transpose(grad_value).astype(BF16)
        dqkv_head[cols, 2 * HEAD : 3 * HEAD] = jnp.transpose(grad_key).astype(BF16)

    def dqkv_copy(k):
        return remote(
            send_dqkv.at[k], recv_dqkv.at[back(k)], dqkv_ss, dqkv_rs.at[back(k)], seq_peer(k)
        )

    def pick_dqkv(k, target):
        low, high = halves(seq_head(k))
        target[k, :HALF] = dqkv_head[low, :]
        target[k, HALF:] = dqkv_head[high, :]

    def send_grad(k, carry):
        pick_dqkv(k, send_dqkv)
        dqkv_copy(k).start()
        return carry

    lax.fori_loop(0, 7, send_grad, 0)
    pick_dqkv(7, recv_dqkv)

    low, high = halves(seq)
    own_stats = jnp.concatenate([row_stats[low, :], row_stats[high, :]], axis=0)
    for j in (7, 0, 1, 2, 3, 4, 5, 6):
        if j < 7:
            centred_copy(back(j)).wait_recv()
        cols = pl.ds(aligned(seq_head(j) * HEAD, HEAD), HEAD)
        normed = (recv_centred[j].astype(F32) + own_stats[:, 4 + j : 5 + j]) * own_stats[:, 1:2]
        mixed[:, cols] = (normed * gate_rows[:, cols].astype(F32)).astype(BF16)
        gp_gate[:, cols] = (grad_mixed[:, cols] * normed * slope_gate[:, cols]).astype(BF16)

    def mixed_block(k):
        return pl.ds(aligned(group_index(k) * HEAD, HEAD), HEAD)

    def mixed_copy(k):
        return remote(
            mixed.at[:, mixed_block(k)],
            mixed_all.at[own_group],
            mixed_ss,
            mixed_rs,
            group_peer(k),
        )

    def send_mixed(k, carry):
        mixed_copy(k).start()
        return carry

    lax.fori_loop(0, 7, send_mixed, 0)
    mixed_all[own_group] = mixed[:, mixed_block(7)]
    lower = (sub <= lane).astype(F32).astype(BF16)
    sums = jnp.zeros((8, HEAD), F32)
    for i in range(8):
        rows = pl.ds(i * HEAD, HEAD)
        for j in range(i + 1):
            running = dot(dscores[rows, pl.ds(j * HEAD, HEAD)], lower)
            for p in range(PACKS):
                last = last_key[i, (j * PACKS + p) * 8 : (j * PACKS + p) * 8 + 8, :]
                lanes = jnp.maximum(last, 0)
                at_limit = jnp.zeros((8, HEAD), F32)
                for a, g in pack_groups(p):
                    at_limit = jnp.where(
                        group == a, pick_lane(running[g * 8 : g * 8 + 8], lanes), at_limit
                    )
                sums = sums + jnp.where(last >= 0, at_limit, 0.0)
    hist_recv[own_piece] = sums

    def hist_copy(k):
        return remote(
            hist_recv.at[own_piece], hist_recv.at[own_piece], hist_ss, hist_rs, piece_peer(k)
        )

    def send_hist(k, carry):
        hist_copy(k).start()
        return carry

    lax.fori_loop(0, 15, send_hist, 0)

    wait_bytes(mixed_all.at[:7], mixed_rs)
    cot_core.wait_recv()
    for g in range(8):
        mixed_t[:, g * ROWS : (g + 1) * ROWS] = jnp.transpose(mixed_all[g])
    for c in range(4):
        cols = slice(c * STEP, (c + 1) * STEP)
        product = sum(
            dot(mixed_t[:, q * STEP : (q + 1) * STEP], cot_pair(cot_all, q, cols)) for q in range(4)
        )
        for half in range(2):
            tile = jnp.transpose(product[:, half * HEAD : (half + 1) * HEAD])
            for t in range(SEQ):
                piece[half * SEQ + t, c * 16 : (c + 1) * 16, :] = jnp.concatenate(
                    [tile[t * 8 : t * 8 + 8], tile[HALF + t * 8 : HALF + t * 8 + 8]], axis=0
                ).astype(BF16)

    def piece_copy(k):
        return remote(
            piece.at[piece_index(k)],
            piece_recv.at[14 - k],
            piece_ss,
            piece_rs,
            piece_peer(k),
        )

    def send_piece(k, carry):
        piece_copy(k).start()
        return carry

    lax.fori_loop(0, 15, send_piece, 0)

    for c in range(4):
        cols = pl.ds(c * STEP, STEP)
        layer_out_rows[:, cols] = dot(mixed[...], w_out[:, cols]).astype(BF16)
        ig_acc[:, cols] = dot_t(gp_gate[...], w_gate[cols, :])
    layer_out_copy = pltpu.make_async_copy(layer_out_rows, layer_out_ref.at[0], store_sem.at[0])
    layer_out_copy.start()

    def add_head(j):
        grad_pre = (recv_dqkv[j].astype(F32) * slope_qkv[j]).astype(BF16)
        for c in range(4):
            cols = pl.ds(c * STEP, STEP)
            ig_acc[:, cols] += dot_t(grad_pre, w_qkv[j, cols, :])

    def take_dqkv(j, carry):
        dqkv_copy(back(j)).wait_recv()
        add_head(j)
        return carry

    add_head(7)
    lax.fori_loop(0, 4, take_dqkv, 0)
    wait_bytes(hist_recv.at[:15], hist_rs)
    heads = jnp.sum(hist_recv[:SEQ] + hist_recv[SEQ:], axis=1) * norm_scale
    hist_all[own_group] = heads

    def all_copy(k):
        return remote(
            hist_all.at[own_group], hist_all.at[own_group], all_ss, all_rs, group_peer(k)
        )

    def send_all(k, carry):
        all_copy(k).start()
        return carry

    lax.fori_loop(0, 7, send_all, 0)

    def take_piece(k, total):
        return total + piece_recv[k].astype(F32)

    wait_bytes(piece_recv, piece_rs)
    total = lax.fori_loop(0, 15, take_piece, piece[own_piece].astype(F32)) * norm_scale
    final_send[...] = total.reshape(8, 8, HEAD)

    def final_copy(k):
        return remote(
            final_send.at[group_index(k)],
            final_recv.at[own_group],
            final_ss,
            final_rs,
            group_peer(k),
        )

    def send_final(k, carry):
        final_copy(k).start()
        return carry

    lax.fori_loop(0, 7, send_final, 0)
    final_recv[own_group] = final_send[own_group]

    lax.fori_loop(4, 7, take_dqkv, 0)
    input_grad_rows[...] = ig_acc[...].astype(BF16)
    input_grad_copy = pltpu.make_async_copy(
        input_grad_rows, input_grad_ref.at[0], store_sem.at[1]
    )
    input_grad_copy.start()

    wait_bytes(hist_all.at[:7], all_rs)
    packed = jnp.sum(hist_all[...], axis=0)
    reached = packed
    for a in range(1, 7):
        reached = reached + pltpu.roll(packed, HEAD - BUCKETS * a, 1)
    every = reached[:, BUCKETS - 1 : BUCKETS]
    reached = jnp.where(lane[:8] == BUCKETS - 1, 0.0, reached)
    before = jnp.where(lane[:8] == 0, every, pltpu.roll(reached, 1, 1))
    bias_grad_ref[...] = (before - reached)[:, :BUCKETS]

    wait_bytes(final_recv.at[:7], final_rs)
    for g in range(8):
        out_grad_ref[:, g * HEAD : (g + 1) * HEAD] = final_recv[g]

    wait_bytes(recv_gn.at[:7], gn_ss)
    wait_bytes(stat_recv.at[:7], stat_ss)
    wait_bytes(recv_centred.at[:7], centred_ss)
    wait_bytes(mixed_all.at[:7], mixed_ss)
    wait_bytes(hist_all.at[:7], all_ss)
    wait_bytes(final_recv.at[:7], final_ss)
    wait_bytes(piece_recv, piece_ss)
    wait_bytes(hist_recv.at[:15], hist_ss)
    wait_bytes(cot_all.at[:3], cot_ss)
    cot_core.wait_send()
    for k in range(4, 7):
        qkv_copy(k).wait_send()
    wait_bytes(recv_dqkv.at[:7], dqkv_ss)
    layer_out_copy.wait()
    input_grad_copy.wait()


def cot_pair(cot_all, q, cols):
    return jnp.concatenate([cot_all[2 * q, :, cols], cot_all[2 * q + 1, :, cols]], axis=0)


def finish(*refs):
    count = len(refs) // 2
    for source, target in zip(refs[:count], refs[count:]):
        target[...] = source[...]


def body(events, in_weight, out_weight, rab_table, lengths, stamps, cotangent):
    dma = pltpu.SemaphoreType.DMA
    vmem = pltpu.VMEM
    scratch = [
        vmem((SEQ, WIDTH, 3 * HEAD), BF16),
        vmem((WIDTH, WIDTH), BF16),
        vmem((WIDTH, WIDTH), BF16),
        vmem((SEQ, ROWS, 3 * HEAD), F32),
        vmem((ROWS, WIDTH), F32),
        vmem((ROWS, WIDTH), BF16),
        vmem((ROWS, WIDTH), F32),
        vmem((ROWS, WIDTH), BF16),
        vmem((SEQ, ROWS, 3 * HEAD), BF16),
        vmem((SEQ, ROWS, 3 * HEAD), BF16),
        vmem((SEQ, ROWS, HEAD), BF16),
        vmem((LEN, HEAD), BF16),
        vmem((LEN, HEAD), BF16),
        vmem((LEN, HEAD), BF16),
        vmem((LEN, HEAD), BF16),
        vmem((LEN, LEN), F32),
        vmem((8, 8 * PACKS, HEAD), jnp.int32),
        vmem((8, 64 * PACKS, HEAD), jnp.int32),
        vmem((LEN, LEN), F32),
        vmem((LEN, LEN), BF16),
        vmem((LEN, LEN), BF16),
        vmem((LEN, HEAD), F32),
        vmem((8, LEN // 2), F32),
        vmem((SEQ, 8, LEN // 2), F32),
        vmem((LEN, HEAD), BF16),
        vmem((LEN, HEAD), F32),
        vmem((LEN, HEAD), BF16),
        vmem((HEAD, LEN), BF16),
        vmem((HEAD, LEN), BF16),
        vmem((SEQ, ROWS, HEAD), BF16),
        vmem((SEQ, ROWS, HEAD), BF16),
        vmem((LEN, 3 * HEAD), BF16),
        vmem((SEQ, ROWS, 3 * HEAD), BF16),
        vmem((SEQ, ROWS, 3 * HEAD), BF16),
        vmem((ROWS, WIDTH), BF16),
        vmem((ROWS, WIDTH), BF16),
        vmem((ROWS, WIDTH), BF16),
        vmem((ROWS, WIDTH), F32),
        vmem((8, ROWS, WIDTH), BF16),
        vmem((8, ROWS, HEAD), BF16),
        vmem((HEAD, 8 * ROWS), BF16),
        vmem((16, HALF, HEAD), BF16),
        vmem((15, HALF, HEAD), BF16),
        vmem((8, 8, HEAD), F32),
        vmem((8, 8, HEAD), F32),
        vmem((16, 8, HEAD), F32),
        vmem((8, 8, HEAD), F32),
        pltpu.SMEM((SEQ, BUCKETS), F32),
        pltpu.SMEM((1, 4), jnp.int32),
        vmem((1, LEN), jnp.int32),
        vmem((ROWS, WIDTH), BF16),
        vmem((ROWS, WIDTH), BF16),
        dma((2,)),
        dma((3,)),
        dma((12,)),
        dma((7,)),
        dma((7,)),
        dma,
        dma((7,)),
        dma,
        dma,
        dma,
        dma((7,)),
        dma,
        dma((7,)),
        dma,
        dma,
        dma,
        dma,
        dma,
        dma,
        dma,
        dma,
        dma,
        dma,
        dma,
        dma,
        dma,
        dma,
    ]
    hbm = pl.BlockSpec(memory_space=pl.ANY)
    local = pl.BlockSpec(memory_space=pltpu.VMEM)
    shapes = (
        jax.ShapeDtypeStruct((1, ROWS, WIDTH), BF16),
        jax.ShapeDtypeStruct((1, ROWS, WIDTH), BF16),
        jax.ShapeDtypeStruct((8, WIDTH), F32),
        jax.ShapeDtypeStruct((SEQ, BUCKETS), F32),
    )
    results = pl.pallas_call(
        kernel,
        out_shape=shapes,
        in_specs=[hbm] * 7,
        out_specs=(hbm, hbm, local, local),
        scratch_shapes=scratch,
        compiler_params=pltpu.CompilerParams(
            collective_id=0, has_side_effects=True, vmem_limit_bytes=60 * 2**20
        ),
    )(events, in_weight, out_weight, rab_table.T, lengths, stamps, cotangent)
    layer_out, input_grad, out_grad, bias_grad = pl.pallas_call(
        finish,
        out_shape=shapes,
        in_specs=[local] * 4,
        out_specs=(local,) * 4,
    )(*results)
    return (layer_out, input_grad, out_grad.T, bias_grad.T)


def solution(mesh):
    placed = (
        P("dp", "seq", None),
        P(),
        P(),
        P(),
        P("dp", None),
        P("dp", None),
        P("dp", "seq", None),
    )
    return jax.shard_map(
        body,
        mesh=mesh,
        in_specs=placed,
        out_specs=(P("dp", "seq", None), P("dp", "seq", None), P(None, ("dp", "seq")), P()),
        check_vma=False,
    )
```

```python
import functools
import math

import jax
import jax.numpy as jnp
from jax import lax
from jax.experimental import pallas as pl
from jax.experimental.pallas import tpu as pltpu
from jax.sharding import PartitionSpec as P

NORM_EPS = 1e-05
HIDDEN = -1e30
MESH = pl.DeviceIdType.MESH
F32 = jnp.float32
BF16 = jnp.bfloat16

SEQ = 8
ROWS = 128
HALF = 64
LEN = 1024
WIDTH = 1024
HEAD = 128
BUCKETS = 18
STEP = 256
PACKS = 3


def dot(left, right):
    return jnp.dot(left, right, preferred_element_type=F32)


def dot_t(left, right):
    return lax.dot_general(left, right, (((1,), (1,)), ((), ())), preferred_element_type=F32)


def sigmoid(values):
    return 0.5 * jnp.tanh(0.5 * values) + 0.5


def pack_groups(p):
    return [(a, 7 * p + a) for a in range(7) if 7 * p + a < 16]


def pick_lane(values, lanes):
    return jnp.take_along_axis(values, lanes, axis=1, mode="promise_in_bounds")


def aligned(value, multiple):
    return pl.multiple_of(value, multiple)


def kernel(
    events_ref,
    in_weight_ref,
    out_weight_ref,
    rab_ref,
    lengths_ref,
    stamps_ref,
    cot_ref,
    layer_out_ref,
    input_grad_ref,
    out_grad_ref,
    bias_grad_ref,
    w_qkv,
    w_gate,
    w_out,
    slope_qkv,
    slope_gate,
    gate_rows,
    grad_mixed,
    gn_rows,
    send_qkv,
    recv_qkv,
    recv_gn,
    query,
    key,
    value,
    gn_head,
    bias,
    limit,
    last_key,
    slope,
    probs,
    dscores,
    attn,
    stat_send,
    stat_recv,
    centred_head,
    row_stats,
    grad_attn,
    query_t,
    grad_attn_t,
    send_centred,
    recv_centred,
    dqkv_head,
    send_dqkv,
    recv_dqkv,
    event_rows,
    mixed,
    gp_gate,
    ig_acc,
    cot_all,
    mixed_all,
    mixed_t,
    piece,
    piece_recv,
    final_send,
    final_recv,
    hist_recv,
    hist_all,
    rab,
    lengths,
    stamps,
    layer_out_rows,
    input_grad_rows,
    store_sem,
    small_sem,
    load_sem,
    qkv_ss,
    qkv_rs,
    gn_ss,
    gn_rs,
    stat_ss,
    stat_rs,
    centred_ss,
    centred_rs,
    dqkv_ss,
    dqkv_rs,
    dv_ss,
    dv_rs,
    cot_ss,
    cot_rs,
    core_ss,
    core_rs,
    mixed_ss,
    mixed_rs,
    final_ss,
    final_rs,
    piece_ss,
    piece_rs,
    hist_ss,
    hist_rs,
    all_ss,
    all_rs,
):
    dp = lax.axis_index("dp")
    seq = lax.axis_index("seq")
    core = lax.rem(dp, 2)
    x_lo = lax.rem(dp // 2, 2)
    y = dp // 4
    score_scale = 1.0 / HEAD**0.5
    norm_scale = 1.0 / math.sqrt(16 * LEN)

    def seq_head(k):
        along_z = lax.rem(seq // 2 + k - 3 * (k // 4), 4)
        return along_z * 2 + lax.rem(seq + k + 1, 2)

    def seq_peer(k):
        return (dp, seq_head(k))

    def back(k):
        upper = k // 4
        return (1 - upper) * lax.rem(8 - k, 4) + upper * (10 - k)

    def y_peer(k):
        return (lax.rem(y + k + 1, 4) * 4 + lax.rem(dp, 4), seq)

    own_group = y * 2 + core

    def group_index(k):
        return lax.rem(own_group + k + 1, 8)

    def group_peer(k):
        other = group_index(k)
        return ((other // 2) * 4 + x_lo * 2 + lax.rem(other, 2), seq)

    own_piece = x_lo * SEQ + seq

    def piece_index(k):
        return lax.rem(own_piece + k + 1, 16)

    def piece_peer(k):
        other = piece_index(k)
        return (y * 4 + (other // SEQ) * 2 + core, lax.rem(other, SEQ))

    core_peer = (dp + 1 - 2 * core, seq)

    def remote(src, dst, ss, rs, device):
        return pltpu.make_async_remote_copy(
            src_ref=src,
            dst_ref=dst,
            send_sem=ss,
            recv_sem=rs,
            device_id=device,
            device_id_type=MESH,
        )

    def wait_bytes(ref, sem):
        pltpu.make_async_copy(ref, ref, sem).wait()

    events_copy = pltpu.make_async_copy(events_ref.at[0], event_rows, load_sem.at[11])
    events_copy.start()

    def weight_copy(k, p):
        head = seq_head(k)
        return pltpu.make_async_copy(
            in_weight_ref.at[:, pl.ds(aligned((p + 1) * WIDTH + head * HEAD, HEAD), HEAD)],
            w_qkv.at[k, :, pl.ds(p * HEAD, HEAD)],
            load_sem.at[k],
        )

    for p in range(3):
        weight_copy(0, p).start()

    small_copies = [
        pltpu.make_async_copy(source, target, small_sem.at[n])
        for n, (source, target) in enumerate(
            ((rab_ref, rab), (lengths_ref, lengths), (stamps_ref, stamps))
        )
    ]
    for copy in small_copies:
        copy.start()

    barrier = pltpu.get_barrier_semaphore()

    def greet_piece(k, carry):
        pl.semaphore_signal(barrier, inc=1, device_id=piece_peer(k), device_id_type=MESH)
        return carry

    def greet_group(k, carry):
        pl.semaphore_signal(barrier, inc=1, device_id=group_peer(k), device_id_type=MESH)
        return carry

    lax.fori_loop(0, 15, greet_piece, 0)
    lax.fori_loop(0, 7, greet_group, 0)

    for k in range(1, SEQ):
        for p in range(3):
            weight_copy(k, p).start()
    out_weight_copy = pltpu.make_async_copy(out_weight_ref, w_out, load_sem.at[8])
    out_weight_copy.start()
    gate_copy = pltpu.make_async_copy(
        in_weight_ref.at[:, pl.ds(0, WIDTH)], w_gate, load_sem.at[9]
    )
    gate_copy.start()
    cot_load = pltpu.make_async_copy(cot_ref.at[0], cot_all.at[own_group], load_sem.at[10])
    cot_load.start()

    events_copy.wait()

    def project(k):
        pltpu.make_async_copy(w_qkv.at[k], w_qkv.at[k], load_sem.at[k]).wait()
        pre = dot(event_rows[...], w_qkv[k])
        sig = sigmoid(pre)
        act = pre * sig
        slope_qkv[k] = sig + act * (1.0 - sig)
        return act.astype(BF16)

    def qkv_copy(k):
        return remote(
            send_qkv.at[k], recv_qkv.at[back(k)], qkv_ss.at[k], qkv_rs.at[back(k)], seq_peer(k)
        )

    def project_keep(k, carry):
        send_qkv[k] = project(k)
        return carry

    def project_send(k, carry):
        send_qkv[k] = project(k)
        qkv_copy(k).start()
        return carry

    def send_kept(k, carry):
        qkv_copy(k).start()
        return carry

    lax.fori_loop(0, 1, project_keep, 0)
    pl.semaphore_wait(barrier, 22)
    lax.fori_loop(0, 1, send_kept, 0)
    lax.fori_loop(1, 5, project_send, 0)
    lax.fori_loop(5, 7, project_keep, 0)
    recv_qkv[7] = project(7)
    qkv_copy(0).wait_send()
    qkv_copy(5).start()

    out_weight_copy.wait()
    gate_copy.wait()
    cot_load.wait()
    for c in range(4):
        cols = pl.ds(c * STEP, STEP)
        pre = dot(event_rows[...], w_gate[:, cols])
        sig = sigmoid(pre)
        act = pre * sig
        slope_gate[:, cols] = sig + act * (1.0 - sig)
        gate_b = act.astype(BF16)
        gate_rows[:, cols] = gate_b
        gm = dot_t(cot_all[own_group], w_out[cols, :])
        grad_mixed[:, cols] = gm
        gn_rows[:, cols] = (gm * gate_b.astype(F32)).astype(BF16)

    def gn_copy(k):
        cols = pl.ds(aligned(seq_head(k) * HEAD, HEAD), HEAD)
        return remote(
            gn_rows.at[:, cols], recv_gn.at[back(k)], gn_ss, gn_rs, seq_peer(k)
        )

    def send_gn(k, carry):
        gn_copy(k).start()
        return carry

    recv_gn[7] = gn_rows[:, pl.ds(aligned(seq * HEAD, HEAD), HEAD)]
    qkv_copy(1).wait_send()
    qkv_copy(6).start()

    def cot_copy(k):
        return remote(
            cot_all.at[own_group], cot_all.at[own_group], cot_ss, cot_rs, y_peer(k)
        )

    def send_cot(k, carry):
        cot_copy(k).start()
        return carry

    lane = lax.broadcasted_iota(jnp.int32, (HEAD, HEAD), 1)
    sub = lax.broadcasted_iota(jnp.int32, (HEAD, HEAD), 0)
    for copy in small_copies:
        copy.wait()
    table_bucket = jnp.minimum(32 - lane[:8], BUCKETS - 1)
    table = jnp.zeros((8, HEAD), F32)
    for b in range(BUCKETS):
        table = jnp.where(table_bucket == b, rab[seq, b], table)
    table = jnp.broadcast_to(table[:1], (HEAD, HEAD))
    group = sum((lane[:8] >= BUCKETS * a).astype(jnp.int32) for a in range(1, 8))
    which = lane - BUCKETS * sum((lane >= BUCKETS * a).astype(jnp.int32) for a in range(1, 8))
    power = jnp.left_shift(1, jnp.minimum(which, BUCKETS - 2))
    end_0 = lengths[0, 0]
    end_1 = end_0 + lengths[0, 1]
    end_2 = end_1 + lengths[0, 2]
    for i in range(8):
        row_stamp = stamps[:, pl.ds(i * HEAD, HEAD)].astype(F32)
        column_stamp = jnp.transpose(jnp.broadcast_to(row_stamp, (HEAD, HEAD))).astype(jnp.int32)
        limits = jnp.where(which < BUCKETS - 1, column_stamp - power, 1 << 30)
        for p in range(PACKS):
            packed = jnp.full((8, HEAD), -1, jnp.int32)
            for a, g in pack_groups(p):
                packed = jnp.where(group == a, limits[g * 8 : g * 8 + 8], packed)
            limit[i, p * 8 : p * 8 + 8, :] = packed
        row_pos = sub + i * HEAD
        first = jnp.where(
            row_pos >= end_2,
            end_2,
            jnp.where(row_pos >= end_1, end_1, jnp.where(row_pos >= end_0, end_0, 0)),
        )
        for j in range(2 * (i // 2) + 2):
            where = (pl.ds(i * HEAD, HEAD), pl.ds(j * HEAD, HEAD))
            key_pos = lane + j * HEAD
            leading = lax.clz(column_stamp - stamps[:, pl.ds(j * HEAD, HEAD)])
            visible = (key_pos >= first) & (key_pos <= row_pos)
            bias[where] = jnp.where(
                visible, pick_lane(table, leading), HIDDEN
            )

    def find_last(i):
        keys = jnp.concatenate(
            [
                jnp.broadcast_to(stamps[:, j * HEAD : (j + 1) * HEAD], (8 * PACKS, HEAD))
                for j in range(i + 1)
            ],
            axis=0,
        )
        most = jnp.concatenate([limit[i]] * (i + 1), axis=0)
        last = jnp.full(most.shape, -1, jnp.int32)
        for step in (64, 32, 16, 8, 4, 2, 1, 1):
            later = last + step
            last = jnp.where(pick_lane(keys, later) <= most, later, last)
        last_key[i, : 8 * PACKS * (i + 1), :] = last

    def halves(block):
        return (
            pl.ds(aligned(block * HALF, HALF), HALF),
            pl.ds(aligned(LEN - HALF - block * HALF, HALF), HALF),
        )

    def place_qkv(j):
        low, high = halves(seq_head(j))
        for at, rows in ((low, slice(0, HALF)), (high, slice(HALF, ROWS))):
            for p, target in enumerate((value, query, key)):
                target[at, :] = recv_qkv[j, rows, p * HEAD : (p + 1) * HEAD]

    def take_qkv(j, carry):
        qkv_copy(back(j)).wait_recv()
        place_qkv(j)
        return carry

    place_qkv(7)
    qkv_copy(2).wait_send()
    qkv_copy(3).wait_send()
    lax.fori_loop(0, 7, send_gn, 0)
    lax.fori_loop(0, 3, send_cot, 0)
    for i in range(8):
        find_last(i)
    lax.fori_loop(0, 7, take_qkv, 0)

    def place_gn(j):
        low, high = halves(seq_head(j))
        gn_head[low, :] = recv_gn[j, :HALF]
        gn_head[high, :] = recv_gn[j, HALF:]

    def take_gn(j, carry):
        place_gn(j)
        return carry

    for i in range(4):
        rows = pl.ds(i * STEP, STEP)
        for j in range(i + 1):
            cols = pl.ds(j * STEP, STEP)
            scores = dot_t(query[rows, :], key[cols, :]) * score_scale + bias[rows, cols]
            sig = sigmoid(scores)
            silu = scores * sig
            probs[rows, cols] = silu.astype(BF16)
            slope[rows, cols] = sig + silu * (1.0 - sig)
        seen = (i + 1) * STEP
        attn[rows, :] = dot(probs[rows, :seen], value[:seen, :])

    place_gn(7)
    wait_bytes(recv_gn.at[:7], gn_rs)
    lax.fori_loop(0, 7, take_gn, 0)

    ones = jnp.ones((HEAD, HEAD), BF16)

    def column_stats(i):
        rows = pl.ds(i * HEAD, HEAD)
        a = attn[rows, :]
        g = gn_head[rows, :].astype(F32)
        mean = jnp.mean(a, axis=1, keepdims=True)
        off = a - mean
        centred_head[rows, :] = off.astype(BF16)
        return (
            mean,
            jnp.sum(off * off, axis=1, keepdims=True),
            dot((g * off).astype(BF16), ones),
            dot(gn_head[rows, :], ones),
        )

    for i in range(4):
        packed = jnp.zeros((HEAD, HEAD), F32)
        for n, column in enumerate(column_stats(i) + column_stats(i + 4)):
            packed = jnp.where(lane == n, column, packed)
        stat_send[:, pl.ds(i * HEAD, HEAD)] = jnp.transpose(packed)[:8]

    def stat_copy(k):
        return remote(
            stat_send, stat_recv.at[back(k)], stat_ss, stat_rs, seq_peer(k)
        )

    def send_stat(k, carry):
        stat_copy(k).start()
        return carry

    lax.fori_loop(0, 7, send_stat, 0)
    stat_recv[7] = stat_send[...]

    def centred_copy(k):
        return remote(
            send_centred.at[k],
            recv_centred.at[back(k)],
            centred_ss,
            centred_rs,
            seq_peer(k),
        )

    def pick_centred(k, target):
        low, high = halves(seq_head(k))
        target[k, :HALF] = centred_head[low, :]
        target[k, HALF:] = centred_head[high, :]

    def send_norm(k, carry):
        pick_centred(k, send_centred)
        centred_copy(k).start()
        return carry

    lax.fori_loop(0, 7, send_norm, 0)
    pick_centred(7, recv_centred)

    for i in range(8):
        rows = pl.ds(i * HEAD, HEAD)
        query_t[:, rows] = jnp.transpose(query[rows, :])

    wait_bytes(stat_recv.at[:7], stat_rs)

    wait_bytes(cot_all.at[:3], cot_rs)
    pairs = cot_all.reshape(4, 2, ROWS, WIDTH)
    cot_core = remote(pairs.at[:, core], pairs.at[:, core], core_ss, core_rs, core_peer)
    cot_core.start()

    for part in range(2):
        rows4 = [[stat_recv[j, part * 4 + n : part * 4 + n + 1, :] for n in range(4)] for j in range(SEQ)]
        mu = sum(r[0] for r in rows4) * (1.0 / SEQ)
        spread = sum(r[1] + HEAD * (r[0] - mu) * (r[0] - mu) for r in rows4)
        inverse = 1.0 / jnp.sqrt(spread * (1.0 / WIDTH) + NORM_EPS)
        along = sum(r[2] + (r[0] - mu) * r[3] for r in rows4) * inverse * (1.0 / WIDTH)
        level = sum(r[3] for r in rows4) * (1.0 / WIDTH)
        columns = jnp.concatenate(
            [mu, inverse, along, level] + [r[0] - mu for r in rows4] + [jnp.zeros_like(mu)] * 4, axis=0
        )
        for i in range(4):
            at = slice(i * HEAD, (i + 1) * HEAD)
            tile = jnp.transpose(
                jnp.concatenate([columns[:, at], jnp.zeros((HEAD - 16, HEAD), F32)], axis=0)
            )
            row_stats[pl.ds((part * 4 + i) * HEAD, HEAD), :] = tile

    for i in range(8):
        rows = pl.ds(i * HEAD, HEAD)
        tile = row_stats[rows, :]
        normed = (attn[rows, :] - tile[:, 0:1]) * tile[:, 1:2]
        grad_attn[rows, :] = (
            (gn_head[rows, :].astype(F32) - tile[:, 3:4] - normed * tile[:, 2:3]) * tile[:, 1:2]
        ).astype(BF16)

    for i in range(8):
        rows = pl.ds(i * HEAD, HEAD)
        grad_attn_t[:, rows] = jnp.transpose(grad_attn[rows, :])
    for j in range(4):
        cols = pl.ds(j * STEP, STEP)
        rest = slice(j * STEP, LEN)
        grad_value = dot(grad_attn_t[:, rest], probs[rest, cols])
        dqkv_head[cols, 0:HEAD] = jnp.transpose(grad_value).astype(BF16)

    def dv_copy(k):
        return remote(
            send_dqkv.at[k, :, pl.ds(0, HEAD)],
            recv_dqkv.at[back(k), :, pl.ds(0, HEAD)],
            dv_ss,
            dv_rs,
            seq_peer(k),
        )

    def pick_dv(k, target):
        low, high = halves(seq_head(k))
        target[k, :HALF, :HEAD] = dqkv_head[low, :HEAD]
        target[k, HALF:, :HEAD] = dqkv_head[high, :HEAD]

    def send_dv(k, carry):
        pick_dv(k, send_dqkv)
        dv_copy(k).start()
        return carry

    lax.fori_loop(0, 7, send_dv, 0)
    pick_dv(7, recv_dqkv)
    for i in range(4):
        rows = pl.ds(i * STEP, STEP)
        for j in range(i + 1):
            cols = pl.ds(j * STEP, STEP)
            ds = dot_t(grad_attn[rows, :], value[cols, :]) * slope[rows, cols]
            dscores[rows, cols] = ds.astype(BF16)
        seen = (i + 1) * STEP
        dqkv_head[rows, HEAD : 2 * HEAD] = (
            dot(dscores[rows, :seen], key[:seen, :]) * score_scale
        ).astype(BF16)
    for j in range(4):
        cols = pl.ds(j * STEP, STEP)
        rest = slice(j * STEP, LEN)
        grad_key = dot(query_t[:, rest], dscores[rest, cols]) * score_scale
        dqkv_head[cols, 2 * HEAD : 3 * HEAD] = jnp.transpose(grad_key).astype(BF16)

    def dqkv_copy(k):
        return remote(
            send_dqkv.at[k, :, pl.ds(HEAD, 2 * HEAD)],
            recv_dqkv.at[back(k), :, pl.ds(HEAD, 2 * HEAD)],
            dqkv_ss,
            dqkv_rs.at[back(k)],
            seq_peer(k),
        )

    def pick_dqkv(k, target):
        low, high = halves(seq_head(k))
        target[k, :HALF, HEAD:] = dqkv_head[low, HEAD:]
        target[k, HALF:, HEAD:] = dqkv_head[high, HEAD:]

    def send_grad(k, carry):
        pick_dqkv(k, send_dqkv)
        dqkv_copy(k).start()
        return carry

    lax.fori_loop(0, 7, send_grad, 0)
    pick_dqkv(7, recv_dqkv)

    low, high = halves(seq)
    own_stats = jnp.concatenate([row_stats[low, :], row_stats[high, :]], axis=0)

    def own_normed(j):
        return (recv_centred[j].astype(F32) + own_stats[:, 4 + j : 5 + j]) * own_stats[:, 1:2]

    def own_columns(j):
        return pl.ds(aligned(seq_head(j) * HEAD, HEAD), HEAD)

    wait_bytes(recv_centred.at[:7], centred_rs)
    for j in range(SEQ):
        cols = own_columns(j)
        mixed[:, cols] = (own_normed(j) * gate_rows[:, cols].astype(F32)).astype(BF16)

    def mixed_block(k):
        return pl.ds(aligned(group_index(k) * HEAD, HEAD), HEAD)

    def mixed_copy(k):
        return remote(
            mixed.at[:, mixed_block(k)],
            mixed_all.at[own_group],
            mixed_ss,
            mixed_rs,
            group_peer(k),
        )

    def send_mixed(k, carry):
        mixed_copy(k).start()
        return carry

    lax.fori_loop(0, 7, send_mixed, 0)
    mixed_all[own_group] = mixed[:, mixed_block(7)]
    for j in range(SEQ):
        cols = own_columns(j)
        gp_gate[:, cols] = (grad_mixed[:, cols] * own_normed(j) * slope_gate[:, cols]).astype(BF16)

    lower = (sub <= lane).astype(F32).astype(BF16)
    sums = jnp.zeros((8, HEAD), F32)
    for i in range(8):
        rows = pl.ds(i * HEAD, HEAD)
        for j in range(i + 1):
            running = dot(dscores[rows, pl.ds(j * HEAD, HEAD)], lower)
            for p in range(PACKS):
                last = last_key[i, (j * PACKS + p) * 8 : (j * PACKS + p) * 8 + 8, :]
                lanes = jnp.maximum(last, 0)
                at_limit = jnp.zeros((8, HEAD), F32)
                for a, g in pack_groups(p):
                    at_limit = jnp.where(
                        group == a, pick_lane(running[g * 8 : g * 8 + 8], lanes), at_limit
                    )
                sums = sums + jnp.where(last >= 0, at_limit, 0.0)
    hist_recv[own_piece] = sums

    def hist_copy(k):
        return remote(
            hist_recv.at[own_piece], hist_recv.at[own_piece], hist_ss, hist_rs, piece_peer(k)
        )

    def send_hist(k, carry):
        hist_copy(k).start()
        return carry

    lax.fori_loop(0, 15, send_hist, 0)

    wait_bytes(mixed_all.at[:7], mixed_rs)
    cot_core.wait_recv()
    for g in range(8):
        mixed_t[:, g * ROWS : (g + 1) * ROWS] = jnp.transpose(mixed_all[g])
    for c in range(4):
        cols = slice(c * STEP, (c + 1) * STEP)
        product = sum(
            dot(mixed_t[:, q * STEP : (q + 1) * STEP], cot_pair(cot_all, q, cols)) for q in range(4)
        )
        for half in range(2):
            tile = jnp.transpose(product[:, half * HEAD : (half + 1) * HEAD])
            for t in range(SEQ):
                piece[half * SEQ + t, c * 16 : (c + 1) * 16, :] = jnp.concatenate(
                    [tile[t * 8 : t * 8 + 8], tile[HALF + t * 8 : HALF + t * 8 + 8]], axis=0
                ).astype(BF16)

    def piece_copy(k):
        return remote(
            piece.at[piece_index(k)],
            piece_recv.at[14 - k],
            piece_ss,
            piece_rs,
            piece_peer(k),
        )

    def send_piece(k, carry):
        piece_copy(k).start()
        return carry

    lax.fori_loop(0, 15, send_piece, 0)

    for c in range(4):
        cols = pl.ds(c * STEP, STEP)
        layer_out_rows[:, cols] = dot(mixed[...], w_out[:, cols]).astype(BF16)
        ig_acc[:, cols] = dot_t(gp_gate[...], w_gate[cols, :])
    layer_out_copy = pltpu.make_async_copy(layer_out_rows, layer_out_ref.at[0], store_sem.at[0])
    layer_out_copy.start()

    def add_head(j):
        grad_pre = (recv_dqkv[j].astype(F32) * slope_qkv[j]).astype(BF16)
        for c in range(4):
            cols = pl.ds(c * STEP, STEP)
            ig_acc[:, cols] += dot_t(grad_pre, w_qkv[j, cols, :])

    def take_dqkv(j, carry):
        dqkv_copy(back(j)).wait_recv()
        add_head(j)
        return carry

    add_head(7)
    wait_bytes(recv_dqkv.at[pl.ds(0, 7), :, pl.ds(0, HEAD)], dv_rs)
    lax.fori_loop(0, 4, take_dqkv, 0)
    wait_bytes(hist_recv.at[:15], hist_rs)
    heads = jnp.sum(hist_recv[:SEQ] + hist_recv[SEQ:], axis=1) * norm_scale
    hist_all[own_group] = heads

    def all_copy(k):
        return remote(
            hist_all.at[own_group], hist_all.at[own_group], all_ss, all_rs, group_peer(k)
        )

    def send_all(k, carry):
        all_copy(k).start()
        return carry

    lax.fori_loop(0, 7, send_all, 0)

    def take_piece(k, total):
        return total + piece_recv[k].astype(F32)

    wait_bytes(piece_recv, piece_rs)
    total = lax.fori_loop(0, 15, take_piece, piece[own_piece].astype(F32)) * norm_scale
    final_send[...] = total.reshape(8, 8, HEAD)

    def final_copy(k):
        return remote(
            final_send.at[group_index(k)],
            final_recv.at[own_group],
            final_ss,
            final_rs,
            group_peer(k),
        )

    def send_final(k, carry):
        final_copy(k).start()
        return carry

    lax.fori_loop(0, 7, send_final, 0)
    final_recv[own_group] = final_send[own_group]

    lax.fori_loop(4, 7, take_dqkv, 0)
    input_grad_rows[...] = ig_acc[...].astype(BF16)
    input_grad_copy = pltpu.make_async_copy(
        input_grad_rows, input_grad_ref.at[0], store_sem.at[1]
    )
    input_grad_copy.start()

    wait_bytes(hist_all.at[:7], all_rs)
    packed = jnp.sum(hist_all[...], axis=0)
    reached = packed
    for a in range(1, 7):
        reached = reached + pltpu.roll(packed, HEAD - BUCKETS * a, 1)
    every = reached[:, BUCKETS - 1 : BUCKETS]
    reached = jnp.where(lane[:8] == BUCKETS - 1, 0.0, reached)
    before = jnp.where(lane[:8] == 0, every, pltpu.roll(reached, 1, 1))
    bias_grad_ref[...] = (before - reached)[:, :BUCKETS]

    wait_bytes(final_recv.at[:7], final_rs)
    for g in range(8):
        out_grad_ref[:, g * HEAD : (g + 1) * HEAD] = final_recv[g]

    wait_bytes(recv_gn.at[:7], gn_ss)
    wait_bytes(stat_recv.at[:7], stat_ss)
    wait_bytes(recv_centred.at[:7], centred_ss)
    wait_bytes(mixed_all.at[:7], mixed_ss)
    wait_bytes(hist_all.at[:7], all_ss)
    wait_bytes(final_recv.at[:7], final_ss)
    wait_bytes(piece_recv, piece_ss)
    wait_bytes(hist_recv.at[:15], hist_ss)
    wait_bytes(cot_all.at[:3], cot_ss)
    cot_core.wait_send()
    for k in range(4, 7):
        qkv_copy(k).wait_send()
    wait_bytes(recv_dqkv.at[pl.ds(0, 7), :, pl.ds(HEAD, 2 * HEAD)], dqkv_ss)
    wait_bytes(recv_dqkv.at[pl.ds(0, 7), :, pl.ds(0, HEAD)], dv_ss)
    layer_out_copy.wait()
    input_grad_copy.wait()


def cot_pair(cot_all, q, cols):
    return jnp.concatenate([cot_all[2 * q, :, cols], cot_all[2 * q + 1, :, cols]], axis=0)


def finish(*refs):
    count = len(refs) // 2
    for source, target in zip(refs[:count], refs[count:]):
        target[...] = source[...]


def body(events, in_weight, out_weight, rab_table, lengths, stamps, cotangent):
    dma = pltpu.SemaphoreType.DMA
    vmem = pltpu.VMEM
    scratch = [
        vmem((SEQ, WIDTH, 3 * HEAD), BF16),
        vmem((WIDTH, WIDTH), BF16),
        vmem((WIDTH, WIDTH), BF16),
        vmem((SEQ, ROWS, 3 * HEAD), F32),
        vmem((ROWS, WIDTH), F32),
        vmem((ROWS, WIDTH), BF16),
        vmem((ROWS, WIDTH), F32),
        vmem((ROWS, WIDTH), BF16),
        vmem((SEQ, ROWS, 3 * HEAD), BF16),
        vmem((SEQ, ROWS, 3 * HEAD), BF16),
        vmem((SEQ, ROWS, HEAD), BF16),
        vmem((LEN, HEAD), BF16),
        vmem((LEN, HEAD), BF16),
        vmem((LEN, HEAD), BF16),
        vmem((LEN, HEAD), BF16),
        vmem((LEN, LEN), F32),
        vmem((8, 8 * PACKS, HEAD), jnp.int32),
        vmem((8, 64 * PACKS, HEAD), jnp.int32),
        vmem((LEN, LEN), F32),
        vmem((LEN, LEN), BF16),
        vmem((LEN, LEN), BF16),
        vmem((LEN, HEAD), F32),
        vmem((8, LEN // 2), F32),
        vmem((SEQ, 8, LEN // 2), F32),
        vmem((LEN, HEAD), BF16),
        vmem((LEN, HEAD), F32),
        vmem((LEN, HEAD), BF16),
        vmem((HEAD, LEN), BF16),
        vmem((HEAD, LEN), BF16),
        vmem((SEQ, ROWS, HEAD), BF16),
        vmem((SEQ, ROWS, HEAD), BF16),
        vmem((LEN, 3 * HEAD), BF16),
        vmem((SEQ, ROWS, 3 * HEAD), BF16),
        vmem((SEQ, ROWS, 3 * HEAD), BF16),
        vmem((ROWS, WIDTH), BF16),
        vmem((ROWS, WIDTH), BF16),
        vmem((ROWS, WIDTH), BF16),
        vmem((ROWS, WIDTH), F32),
        vmem((8, ROWS, WIDTH), BF16),
        vmem((8, ROWS, HEAD), BF16),
        vmem((HEAD, 8 * ROWS), BF16),
        vmem((16, HALF, HEAD), BF16),
        vmem((15, HALF, HEAD), BF16),
        vmem((8, 8, HEAD), F32),
        vmem((8, 8, HEAD), F32),
        vmem((16, 8, HEAD), F32),
        vmem((8, 8, HEAD), F32),
        pltpu.SMEM((SEQ, BUCKETS), F32),
        pltpu.SMEM((1, 4), jnp.int32),
        vmem((1, LEN), jnp.int32),
        vmem((ROWS, WIDTH), BF16),
        vmem((ROWS, WIDTH), BF16),
        dma((2,)),
        dma((3,)),
        dma((12,)),
        dma((7,)),
        dma((7,)),
        dma,
        dma,
        dma,
        dma,
        dma,
        dma,
        dma,
        dma((7,)),
        dma,
        dma,
        dma,
        dma,
        dma,
        dma,
        dma,
        dma,
        dma,
        dma,
        dma,
        dma,
        dma,
        dma,
        dma,
        dma,
    ]
    hbm = pl.BlockSpec(memory_space=pl.ANY)
    local = pl.BlockSpec(memory_space=pltpu.VMEM)
    shapes = (
        jax.ShapeDtypeStruct((1, ROWS, WIDTH), BF16),
        jax.ShapeDtypeStruct((1, ROWS, WIDTH), BF16),
        jax.ShapeDtypeStruct((8, WIDTH), F32),
        jax.ShapeDtypeStruct((SEQ, BUCKETS), F32),
    )
    results = pl.pallas_call(
        kernel,
        out_shape=shapes,
        in_specs=[hbm] * 7,
        out_specs=(hbm, hbm, local, local),
        scratch_shapes=scratch,
        compiler_params=pltpu.CompilerParams(
            collective_id=0, has_side_effects=True, vmem_limit_bytes=60 * 2**20
        ),
    )(events, in_weight, out_weight, rab_table.T, lengths, stamps, cotangent)
    layer_out, input_grad, out_grad, bias_grad = pl.pallas_call(
        finish,
        out_shape=shapes,
        in_specs=[local] * 4,
        out_specs=(local,) * 4,
    )(*results)
    return (layer_out, input_grad, out_grad.T, bias_grad.T)


def solution(mesh):
    placed = (
        P("dp", "seq", None),
        P(),
        P(),
        P(),
        P("dp", None),
        P("dp", None),
        P("dp", "seq", None),
    )
    return jax.shard_map(
        body,
        mesh=mesh,
        in_specs=placed,
        out_specs=(P("dp", "seq", None), P("dp", "seq", None), P(None, ("dp", "seq")), P()),
        check_vma=False,
    )
```

```python
import functools
import math

import jax
import jax.numpy as jnp
from jax import lax
from jax.experimental import pallas as pl
from jax.experimental.pallas import tpu as pltpu
from jax.sharding import PartitionSpec as P

NORM_EPS = 1e-05
HIDDEN = -1e30
MESH = pl.DeviceIdType.MESH
F32 = jnp.float32
BF16 = jnp.bfloat16

SEQ = 8
ROWS = 128
HALF = 64
LEN = 1024
WIDTH = 1024
HEAD = 128
BUCKETS = 18
STEP = 256
PACKS = 3


def dot(left, right):
    return jnp.dot(left, right, preferred_element_type=F32)


def dot_t(left, right):
    return lax.dot_general(left, right, (((1,), (1,)), ((), ())), preferred_element_type=F32)


def sigmoid(values):
    return 0.5 * jnp.tanh(0.5 * values) + 0.5


def pack_groups(p):
    return [(a, 7 * p + a) for a in range(7) if 7 * p + a < 16]


def pick_lane(values, lanes):
    return jnp.take_along_axis(values, lanes, axis=1, mode="promise_in_bounds")


def aligned(value, multiple):
    return pl.multiple_of(value, multiple)


def kernel(
    events_ref,
    in_weight_ref,
    out_weight_ref,
    rab_ref,
    lengths_ref,
    stamps_ref,
    cot_ref,
    layer_out_ref,
    input_grad_ref,
    out_grad_ref,
    bias_grad_ref,
    w_qkv,
    w_gate,
    w_out,
    slope_qkv,
    slope_gate,
    gate_rows,
    grad_mixed,
    gn_rows,
    send_qkv,
    recv_qkv,
    recv_gn,
    query,
    key,
    value,
    gn_head,
    bias,
    limit,
    last_key,
    slope,
    probs,
    dscores,
    attn,
    stat_send,
    stat_recv,
    centred_head,
    row_stats,
    grad_attn,
    query_t,
    grad_attn_t,
    send_centred,
    recv_centred,
    dqkv_head,
    send_dqkv,
    recv_dqkv,
    event_rows,
    mixed,
    gp_gate,
    ig_acc,
    cot_all,
    mixed_all,
    mixed_t,
    piece,
    piece_recv,
    final_send,
    final_recv,
    hist_recv,
    hist_all,
    rab,
    lengths,
    stamps,
    layer_out_rows,
    input_grad_rows,
    store_sem,
    small_sem,
    load_sem,
    qkv_ss,
    qkv_rs,
    gn_ss,
    gn_rs,
    stat_ss,
    stat_rs,
    centred_ss,
    centred_rs,
    dqkv_ss,
    dqkv_rs,
    dv_ss,
    dv_rs,
    v_ss,
    v_rs,
    cot_ss,
    cot_rs,
    core_ss,
    core_rs,
    mixed_ss,
    mixed_rs,
    final_ss,
    final_rs,
    piece_ss,
    piece_rs,
    hist_ss,
    hist_rs,
    all_ss,
    all_rs,
):
    dp = lax.axis_index("dp")
    seq = lax.axis_index("seq")
    core = lax.rem(dp, 2)
    x_lo = lax.rem(dp // 2, 2)
    y = dp // 4
    score_scale = 1.0 / HEAD**0.5
    norm_scale = 1.0 / math.sqrt(16 * LEN)

    def seq_head(k):
        along_z = lax.rem(seq // 2 + k - 3 * (k // 4), 4)
        return along_z * 2 + lax.rem(seq + k + 1, 2)

    def seq_peer(k):
        return (dp, seq_head(k))

    def back(k):
        upper = k // 4
        return (1 - upper) * lax.rem(8 - k, 4) + upper * (10 - k)

    def y_peer(k):
        return (lax.rem(y + k + 1, 4) * 4 + lax.rem(dp, 4), seq)

    own_group = y * 2 + core

    def group_index(k):
        return lax.rem(own_group + k + 1, 8)

    def group_peer(k):
        other = group_index(k)
        return ((other // 2) * 4 + x_lo * 2 + lax.rem(other, 2), seq)

    own_piece = x_lo * SEQ + seq

    def piece_index(k):
        return lax.rem(own_piece + k + 1, 16)

    def piece_peer(k):
        other = piece_index(k)
        return (y * 4 + (other // SEQ) * 2 + core, lax.rem(other, SEQ))

    core_peer = (dp + 1 - 2 * core, seq)

    def remote(src, dst, ss, rs, device):
        return pltpu.make_async_remote_copy(
            src_ref=src,
            dst_ref=dst,
            send_sem=ss,
            recv_sem=rs,
            device_id=device,
            device_id_type=MESH,
        )

    def wait_bytes(ref, sem):
        pltpu.make_async_copy(ref, ref, sem).wait()

    events_copy = pltpu.make_async_copy(events_ref.at[0], event_rows, load_sem.at[11])
    events_copy.start()

    def weight_copy(k, p):
        head = seq_head(k)
        return pltpu.make_async_copy(
            in_weight_ref.at[:, pl.ds(aligned((p + 1) * WIDTH + head * HEAD, HEAD), HEAD)],
            w_qkv.at[k, :, pl.ds(p * HEAD, HEAD)],
            load_sem.at[k],
        )

    for p in range(3):
        weight_copy(0, p).start()

    small_copies = [
        pltpu.make_async_copy(source, target, small_sem.at[n])
        for n, (source, target) in enumerate(
            ((rab_ref, rab), (lengths_ref, lengths), (stamps_ref, stamps))
        )
    ]
    for copy in small_copies:
        copy.start()

    barrier = pltpu.get_barrier_semaphore()

    def greet_piece(k, carry):
        pl.semaphore_signal(barrier, inc=1, device_id=piece_peer(k), device_id_type=MESH)
        return carry

    def greet_group(k, carry):
        pl.semaphore_signal(barrier, inc=1, device_id=group_peer(k), device_id_type=MESH)
        return carry

    lax.fori_loop(0, 15, greet_piece, 0)
    lax.fori_loop(0, 7, greet_group, 0)

    for k in range(1, SEQ):
        for p in range(3):
            weight_copy(k, p).start()
    out_weight_copy = pltpu.make_async_copy(out_weight_ref, w_out, load_sem.at[8])
    out_weight_copy.start()
    gate_copy = pltpu.make_async_copy(
        in_weight_ref.at[:, pl.ds(0, WIDTH)], w_gate, load_sem.at[9]
    )
    gate_copy.start()
    cot_load = pltpu.make_async_copy(cot_ref.at[0], cot_all.at[own_group], load_sem.at[10])
    cot_load.start()

    events_copy.wait()

    def project(k):
        pltpu.make_async_copy(w_qkv.at[k], w_qkv.at[k], load_sem.at[k]).wait()
        pre = dot(event_rows[...], w_qkv[k])
        sig = sigmoid(pre)
        act = pre * sig
        slope_qkv[k] = sig + act * (1.0 - sig)
        return act.astype(BF16)

    def qkv_copy(k):
        return remote(
            send_qkv.at[k, :, pl.ds(HEAD, 2 * HEAD)],
            recv_qkv.at[back(k), :, pl.ds(HEAD, 2 * HEAD)],
            qkv_ss,
            qkv_rs.at[back(k)],
            seq_peer(k),
        )

    def v_copy(k):
        return remote(
            send_qkv.at[k, :, pl.ds(0, HEAD)],
            recv_qkv.at[back(k), :, pl.ds(0, HEAD)],
            v_ss,
            v_rs,
            seq_peer(k),
        )

    def send_v(k, carry):
        v_copy(k).start()
        return carry

    def project_keep(k, carry):
        send_qkv[k] = project(k)
        return carry

    def project_send(k, carry):
        send_qkv[k] = project(k)
        qkv_copy(k).start()
        return carry

    def send_kept(k, carry):
        qkv_copy(k).start()
        return carry

    lax.fori_loop(0, 1, project_keep, 0)
    pl.semaphore_wait(barrier, 22)
    lax.fori_loop(0, 1, send_kept, 0)
    lax.fori_loop(1, 7, project_send, 0)
    recv_qkv[7] = project(7)
    lax.fori_loop(0, 7, send_v, 0)

    out_weight_copy.wait()
    gate_copy.wait()
    cot_load.wait()
    for c in range(4):
        cols = pl.ds(c * STEP, STEP)
        pre = dot(event_rows[...], w_gate[:, cols])
        sig = sigmoid(pre)
        act = pre * sig
        slope_gate[:, cols] = sig + act * (1.0 - sig)
        gate_b = act.astype(BF16)
        gate_rows[:, cols] = gate_b
        gm = dot_t(cot_all[own_group], w_out[cols, :])
        grad_mixed[:, cols] = gm
        gn_rows[:, cols] = (gm * gate_b.astype(F32)).astype(BF16)

    def gn_copy(k):
        cols = pl.ds(aligned(seq_head(k) * HEAD, HEAD), HEAD)
        return remote(
            gn_rows.at[:, cols], recv_gn.at[back(k)], gn_ss, gn_rs, seq_peer(k)
        )

    def send_gn(k, carry):
        gn_copy(k).start()
        return carry

    recv_gn[7] = gn_rows[:, pl.ds(aligned(seq * HEAD, HEAD), HEAD)]

    def cot_copy(k):
        return remote(
            cot_all.at[own_group], cot_all.at[own_group], cot_ss, cot_rs, y_peer(k)
        )

    def send_cot(k, carry):
        cot_copy(k).start()
        return carry

    lane = lax.broadcasted_iota(jnp.int32, (HEAD, HEAD), 1)
    sub = lax.broadcasted_iota(jnp.int32, (HEAD, HEAD), 0)
    for copy in small_copies:
        copy.wait()
    table_bucket = jnp.minimum(32 - lane[:8], BUCKETS - 1)
    table = jnp.zeros((8, HEAD), F32)
    for b in range(BUCKETS):
        table = jnp.where(table_bucket == b, rab[seq, b], table)
    table = jnp.broadcast_to(table[:1], (HEAD, HEAD))
    group = sum((lane[:8] >= BUCKETS * a).astype(jnp.int32) for a in range(1, 8))
    which = lane - BUCKETS * sum((lane >= BUCKETS * a).astype(jnp.int32) for a in range(1, 8))
    power = jnp.left_shift(1, jnp.minimum(which, BUCKETS - 2))
    end_0 = lengths[0, 0]
    end_1 = end_0 + lengths[0, 1]
    end_2 = end_1 + lengths[0, 2]
    for i in range(8):
        row_stamp = stamps[:, pl.ds(i * HEAD, HEAD)].astype(F32)
        column_stamp = jnp.transpose(jnp.broadcast_to(row_stamp, (HEAD, HEAD))).astype(jnp.int32)
        limits = jnp.where(which < BUCKETS - 1, column_stamp - power, 1 << 30)
        for p in range(PACKS):
            packed = jnp.full((8, HEAD), -1, jnp.int32)
            for a, g in pack_groups(p):
                packed = jnp.where(group == a, limits[g * 8 : g * 8 + 8], packed)
            limit[i, p * 8 : p * 8 + 8, :] = packed
        row_pos = sub + i * HEAD
        first = jnp.where(
            row_pos >= end_2,
            end_2,
            jnp.where(row_pos >= end_1, end_1, jnp.where(row_pos >= end_0, end_0, 0)),
        )
        for j in range(2 * (i // 2) + 2):
            where = (pl.ds(i * HEAD, HEAD), pl.ds(j * HEAD, HEAD))
            key_pos = lane + j * HEAD
            leading = lax.clz(column_stamp - stamps[:, pl.ds(j * HEAD, HEAD)])
            visible = (key_pos >= first) & (key_pos <= row_pos)
            bias[where] = jnp.where(
                visible, pick_lane(table, leading), HIDDEN
            )

    def find_last(i):
        keys = jnp.concatenate(
            [
                jnp.broadcast_to(stamps[:, j * HEAD : (j + 1) * HEAD], (8 * PACKS, HEAD))
                for j in range(i + 1)
            ],
            axis=0,
        )
        most = jnp.concatenate([limit[i]] * (i + 1), axis=0)
        last = jnp.full(most.shape, -1, jnp.int32)
        for step in (64, 32, 16, 8, 4, 2, 1, 1):
            later = last + step
            last = jnp.where(pick_lane(keys, later) <= most, later, last)
        last_key[i, : 8 * PACKS * (i + 1), :] = last

    def halves(block):
        return (
            pl.ds(aligned(block * HALF, HALF), HALF),
            pl.ds(aligned(LEN - HALF - block * HALF, HALF), HALF),
        )

    def place_qkv(j):
        low, high = halves(seq_head(j))
        for at, rows in ((low, slice(0, HALF)), (high, slice(HALF, ROWS))):
            query[at, :] = recv_qkv[j, rows, HEAD : 2 * HEAD]
            key[at, :] = recv_qkv[j, rows, 2 * HEAD :]

    def take_qkv(j, carry):
        qkv_copy(back(j)).wait_recv()
        place_qkv(j)
        return carry

    place_qkv(7)
    lax.fori_loop(0, 7, send_gn, 0)
    lax.fori_loop(0, 3, send_cot, 0)
    for i in range(8):
        find_last(i)
    lax.fori_loop(0, 7, take_qkv, 0)

    def place_gn(j):
        low, high = halves(seq_head(j))
        gn_head[low, :] = recv_gn[j, :HALF]
        gn_head[high, :] = recv_gn[j, HALF:]

    def take_gn(j, carry):
        place_gn(j)
        return carry

    for i in range(4):
        rows = pl.ds(i * STEP, STEP)
        for j in range(i + 1):
            cols = pl.ds(j * STEP, STEP)
            scores = dot_t(query[rows, :], key[cols, :]) * score_scale + bias[rows, cols]
            sig = sigmoid(scores)
            silu = scores * sig
            probs[rows, cols] = silu.astype(BF16)
            slope[rows, cols] = sig + silu * (1.0 - sig)

    def place_v(j, carry):
        low, high = halves(seq_head(j))
        value[low, :] = recv_qkv[j, :HALF, :HEAD]
        value[high, :] = recv_qkv[j, HALF:, :HEAD]
        return carry

    wait_bytes(recv_qkv.at[pl.ds(0, 7), :, pl.ds(0, HEAD)], v_rs)
    lax.fori_loop(0, SEQ, place_v, 0)
    for i in range(4):
        rows = pl.ds(i * STEP, STEP)
        seen = (i + 1) * STEP
        attn[rows, :] = dot(probs[rows, :seen], value[:seen, :])

    place_gn(7)
    wait_bytes(recv_gn.at[:7], gn_rs)
    lax.fori_loop(0, 7, take_gn, 0)

    ones = jnp.ones((HEAD, HEAD), BF16)

    def column_stats(i):
        rows = pl.ds(i * HEAD, HEAD)
        a = attn[rows, :]
        g = gn_head[rows, :].astype(F32)
        mean = jnp.mean(a, axis=1, keepdims=True)
        off = a - mean
        centred_head[rows, :] = off.astype(BF16)
        return (
            mean,
            jnp.sum(off * off, axis=1, keepdims=True),
            dot((g * off).astype(BF16), ones),
            dot(gn_head[rows, :], ones),
        )

    for i in range(4):
        packed = jnp.zeros((HEAD, HEAD), F32)
        for n, column in enumerate(column_stats(i) + column_stats(i + 4)):
            packed = jnp.where(lane == n, column, packed)
        stat_send[:, pl.ds(i * HEAD, HEAD)] = jnp.transpose(packed)[:8]

    def stat_copy(k):
        return remote(
            stat_send, stat_recv.at[back(k)], stat_ss, stat_rs, seq_peer(k)
        )

    def send_stat(k, carry):
        stat_copy(k).start()
        return carry

    lax.fori_loop(0, 7, send_stat, 0)
    stat_recv[7] = stat_send[...]

    def centred_copy(k):
        return remote(
            send_centred.at[k],
            recv_centred.at[back(k)],
            centred_ss,
            centred_rs,
            seq_peer(k),
        )

    def pick_centred(k, target):
        low, high = halves(seq_head(k))
        target[k, :HALF] = centred_head[low, :]
        target[k, HALF:] = centred_head[high, :]

    def send_norm(k, carry):
        pick_centred(k, send_centred)
        centred_copy(k).start()
        return carry

    lax.fori_loop(0, 7, send_norm, 0)
    pick_centred(7, recv_centred)

    for i in range(8):
        rows = pl.ds(i * HEAD, HEAD)
        query_t[:, rows] = jnp.transpose(query[rows, :])

    wait_bytes(stat_recv.at[:7], stat_rs)

    wait_bytes(cot_all.at[:3], cot_rs)
    pairs = cot_all.reshape(4, 2, ROWS, WIDTH)
    cot_core = remote(pairs.at[:, core], pairs.at[:, core], core_ss, core_rs, core_peer)
    cot_core.start()

    for part in range(2):
        rows4 = [[stat_recv[j, part * 4 + n : part * 4 + n + 1, :] for n in range(4)] for j in range(SEQ)]
        mu = sum(r[0] for r in rows4) * (1.0 / SEQ)
        spread = sum(r[1] + HEAD * (r[0] - mu) * (r[0] - mu) for r in rows4)
        inverse = 1.0 / jnp.sqrt(spread * (1.0 / WIDTH) + NORM_EPS)
        along = sum(r[2] + (r[0] - mu) * r[3] for r in rows4) * inverse * (1.0 / WIDTH)
        level = sum(r[3] for r in rows4) * (1.0 / WIDTH)
        columns = jnp.concatenate(
            [mu, inverse, along, level] + [r[0] - mu for r in rows4] + [jnp.zeros_like(mu)] * 4, axis=0
        )
        for i in range(4):
            at = slice(i * HEAD, (i + 1) * HEAD)
            tile = jnp.transpose(
                jnp.concatenate([columns[:, at], jnp.zeros((HEAD - 16, HEAD), F32)], axis=0)
            )
            row_stats[pl.ds((part * 4 + i) * HEAD, HEAD), :] = tile

    for i in range(8):
        rows = pl.ds(i * HEAD, HEAD)
        tile = row_stats[rows, :]
        normed = (attn[rows, :] - tile[:, 0:1]) * tile[:, 1:2]
        grad_attn[rows, :] = (
            (gn_head[rows, :].astype(F32) - tile[:, 3:4] - normed * tile[:, 2:3]) * tile[:, 1:2]
        ).astype(BF16)

    for i in range(8):
        rows = pl.ds(i * HEAD, HEAD)
        grad_attn_t[:, rows] = jnp.transpose(grad_attn[rows, :])
    for j in range(4):
        cols = pl.ds(j * STEP, STEP)
        rest = slice(j * STEP, LEN)
        grad_value = dot(grad_attn_t[:, rest], probs[rest, cols])
        dqkv_head[cols, 0:HEAD] = jnp.transpose(grad_value).astype(BF16)

    def dv_copy(k):
        return remote(
            send_dqkv.at[k, :, pl.ds(0, HEAD)],
            recv_dqkv.at[back(k), :, pl.ds(0, HEAD)],
            dv_ss,
            dv_rs,
            seq_peer(k),
        )

    def pick_dv(k, target):
        low, high = halves(seq_head(k))
        target[k, :HALF, :HEAD] = dqkv_head[low, :HEAD]
        target[k, HALF:, :HEAD] = dqkv_head[high, :HEAD]

    def send_dv(k, carry):
        pick_dv(k, send_dqkv)
        dv_copy(k).start()
        return carry

    lax.fori_loop(0, 7, send_dv, 0)
    pick_dv(7, recv_dqkv)
    for i in range(4):
        rows = pl.ds(i * STEP, STEP)
        for j in range(i + 1):
            cols = pl.ds(j * STEP, STEP)
            ds = dot_t(grad_attn[rows, :], value[cols, :]) * slope[rows, cols]
            dscores[rows, cols] = ds.astype(BF16)
        seen = (i + 1) * STEP
        dqkv_head[rows, HEAD : 2 * HEAD] = (
            dot(dscores[rows, :seen], key[:seen, :]) * score_scale
        ).astype(BF16)
    for j in range(4):
        cols = pl.ds(j * STEP, STEP)
        rest = slice(j * STEP, LEN)
        grad_key = dot(query_t[:, rest], dscores[rest, cols]) * score_scale
        dqkv_head[cols, 2 * HEAD : 3 * HEAD] = jnp.transpose(grad_key).astype(BF16)

    def dqkv_copy(k):
        return remote(
            send_dqkv.at[k, :, pl.ds(HEAD, 2 * HEAD)],
            recv_dqkv.at[back(k), :, pl.ds(HEAD, 2 * HEAD)],
            dqkv_ss,
            dqkv_rs.at[back(k)],
            seq_peer(k),
        )

    def pick_dqkv(k, target):
        low, high = halves(seq_head(k))
        target[k, :HALF, HEAD:] = dqkv_head[low, HEAD:]
        target[k, HALF:, HEAD:] = dqkv_head[high, HEAD:]

    def send_grad(k, carry):
        pick_dqkv(k, send_dqkv)
        dqkv_copy(k).start()
        return carry

    lax.fori_loop(0, 7, send_grad, 0)
    pick_dqkv(7, recv_dqkv)

    low, high = halves(seq)
    own_stats = jnp.concatenate([row_stats[low, :], row_stats[high, :]], axis=0)

    def own_normed(j):
        return (recv_centred[j].astype(F32) + own_stats[:, 4 + j : 5 + j]) * own_stats[:, 1:2]

    def own_columns(j):
        return pl.ds(aligned(seq_head(j) * HEAD, HEAD), HEAD)

    wait_bytes(recv_centred.at[:7], centred_rs)
    for j in range(SEQ):
        cols = own_columns(j)
        mixed[:, cols] = (own_normed(j) * gate_rows[:, cols].astype(F32)).astype(BF16)

    def mixed_block(k):
        return pl.ds(aligned(group_index(k) * HEAD, HEAD), HEAD)

    def mixed_copy(k):
        return remote(
            mixed.at[:, mixed_block(k)],
            mixed_all.at[own_group],
            mixed_ss,
            mixed_rs,
            group_peer(k),
        )

    def send_mixed(k, carry):
        mixed_copy(k).start()
        return carry

    lax.fori_loop(0, 7, send_mixed, 0)
    mixed_all[own_group] = mixed[:, mixed_block(7)]
    for j in range(SEQ):
        cols = own_columns(j)
        gp_gate[:, cols] = (grad_mixed[:, cols] * own_normed(j) * slope_gate[:, cols]).astype(BF16)

    lower = (sub <= lane).astype(F32).astype(BF16)
    sums = jnp.zeros((8, HEAD), F32)
    for i in range(8):
        rows = pl.ds(i * HEAD, HEAD)
        for j in range(i + 1):
            running = dot(dscores[rows, pl.ds(j * HEAD, HEAD)], lower)
            for p in range(PACKS):
                last = last_key[i, (j * PACKS + p) * 8 : (j * PACKS + p) * 8 + 8, :]
                lanes = jnp.maximum(last, 0)
                at_limit = jnp.zeros((8, HEAD), F32)
                for a, g in pack_groups(p):
                    at_limit = jnp.where(
                        group == a, pick_lane(running[g * 8 : g * 8 + 8], lanes), at_limit
                    )
                sums = sums + jnp.where(last >= 0, at_limit, 0.0)
    hist_recv[own_piece] = sums

    def hist_copy(k):
        return remote(
            hist_recv.at[own_piece], hist_recv.at[own_piece], hist_ss, hist_rs, piece_peer(k)
        )

    def send_hist(k, carry):
        hist_copy(k).start()
        return carry

    lax.fori_loop(0, 15, send_hist, 0)

    for c in range(4):
        cols = pl.ds(c * STEP, STEP)
        layer_out_rows[:, cols] = dot(mixed[...], w_out[:, cols]).astype(BF16)
        ig_acc[:, cols] = dot_t(gp_gate[...], w_gate[cols, :])
    layer_out_copy = pltpu.make_async_copy(layer_out_rows, layer_out_ref.at[0], store_sem.at[0])
    layer_out_copy.start()

    wait_bytes(mixed_all.at[:7], mixed_rs)
    cot_core.wait_recv()
    for g in range(8):
        mixed_t[:, g * ROWS : (g + 1) * ROWS] = jnp.transpose(mixed_all[g])
    for c in range(4):
        cols = slice(c * STEP, (c + 1) * STEP)
        product = sum(
            dot(mixed_t[:, q * STEP : (q + 1) * STEP], cot_pair(cot_all, q, cols)) for q in range(4)
        )
        for half in range(2):
            tile = jnp.transpose(product[:, half * HEAD : (half + 1) * HEAD])
            for t in range(SEQ):
                piece[half * SEQ + t, c * 16 : (c + 1) * 16, :] = jnp.concatenate(
                    [tile[t * 8 : t * 8 + 8], tile[HALF + t * 8 : HALF + t * 8 + 8]], axis=0
                ).astype(BF16)

    def piece_copy(k):
        return remote(
            piece.at[piece_index(k)],
            piece_recv.at[14 - k],
            piece_ss,
            piece_rs,
            piece_peer(k),
        )

    def send_piece(k, carry):
        piece_copy(k).start()
        return carry

    lax.fori_loop(0, 15, send_piece, 0)

    def add_head(j):
        grad_pre = (recv_dqkv[j].astype(F32) * slope_qkv[j]).astype(BF16)
        for c in range(4):
            cols = pl.ds(c * STEP, STEP)
            ig_acc[:, cols] += dot_t(grad_pre, w_qkv[j, cols, :])

    def take_dqkv(j, carry):
        dqkv_copy(back(j)).wait_recv()
        add_head(j)
        return carry

    add_head(7)
    wait_bytes(recv_dqkv.at[pl.ds(0, 7), :, pl.ds(0, HEAD)], dv_rs)
    lax.fori_loop(0, 4, take_dqkv, 0)
    wait_bytes(hist_recv.at[:15], hist_rs)
    heads = jnp.sum(hist_recv[:SEQ] + hist_recv[SEQ:], axis=1) * norm_scale
    hist_all[own_group] = heads

    def all_copy(k):
        return remote(
            hist_all.at[own_group], hist_all.at[own_group], all_ss, all_rs, group_peer(k)
        )

    def send_all(k, carry):
        all_copy(k).start()
        return carry

    lax.fori_loop(0, 7, send_all, 0)

    def take_piece(k, total):
        return total + piece_recv[k].astype(F32)

    wait_bytes(piece_recv, piece_rs)
    total = lax.fori_loop(0, 15, take_piece, piece[own_piece].astype(F32)) * norm_scale
    final_send[...] = total.reshape(8, 8, HEAD)

    def final_copy(k):
        return remote(
            final_send.at[group_index(k)],
            final_recv.at[own_group],
            final_ss,
            final_rs,
            group_peer(k),
        )

    def send_final(k, carry):
        final_copy(k).start()
        return carry

    lax.fori_loop(0, 7, send_final, 0)
    final_recv[own_group] = final_send[own_group]

    lax.fori_loop(4, 7, take_dqkv, 0)
    input_grad_rows[...] = ig_acc[...].astype(BF16)
    input_grad_copy = pltpu.make_async_copy(
        input_grad_rows, input_grad_ref.at[0], store_sem.at[1]
    )
    input_grad_copy.start()

    wait_bytes(hist_all.at[:7], all_rs)
    packed = jnp.sum(hist_all[...], axis=0)
    reached = packed
    for a in range(1, 7):
        reached = reached + pltpu.roll(packed, HEAD - BUCKETS * a, 1)
    every = reached[:, BUCKETS - 1 : BUCKETS]
    reached = jnp.where(lane[:8] == BUCKETS - 1, 0.0, reached)
    before = jnp.where(lane[:8] == 0, every, pltpu.roll(reached, 1, 1))
    bias_grad_ref[...] = (before - reached)[:, :BUCKETS]

    wait_bytes(final_recv.at[:7], final_rs)
    for g in range(8):
        out_grad_ref[:, g * HEAD : (g + 1) * HEAD] = final_recv[g]

    wait_bytes(recv_gn.at[:7], gn_ss)
    wait_bytes(stat_recv.at[:7], stat_ss)
    wait_bytes(recv_centred.at[:7], centred_ss)
    wait_bytes(mixed_all.at[:7], mixed_ss)
    wait_bytes(hist_all.at[:7], all_ss)
    wait_bytes(final_recv.at[:7], final_ss)
    wait_bytes(piece_recv, piece_ss)
    wait_bytes(hist_recv.at[:15], hist_ss)
    wait_bytes(cot_all.at[:3], cot_ss)
    cot_core.wait_send()
    wait_bytes(recv_qkv.at[pl.ds(0, 7), :, pl.ds(HEAD, 2 * HEAD)], qkv_ss)
    wait_bytes(recv_qkv.at[pl.ds(0, 7), :, pl.ds(0, HEAD)], v_ss)
    wait_bytes(recv_dqkv.at[pl.ds(0, 7), :, pl.ds(HEAD, 2 * HEAD)], dqkv_ss)
    wait_bytes(recv_dqkv.at[pl.ds(0, 7), :, pl.ds(0, HEAD)], dv_ss)
    layer_out_copy.wait()
    input_grad_copy.wait()


def cot_pair(cot_all, q, cols):
    return jnp.concatenate([cot_all[2 * q, :, cols], cot_all[2 * q + 1, :, cols]], axis=0)


def finish(*refs):
    count = len(refs) // 2
    for source, target in zip(refs[:count], refs[count:]):
        target[...] = source[...]


def body(events, in_weight, out_weight, rab_table, lengths, stamps, cotangent):
    dma = pltpu.SemaphoreType.DMA
    vmem = pltpu.VMEM
    scratch = [
        vmem((SEQ, WIDTH, 3 * HEAD), BF16),
        vmem((WIDTH, WIDTH), BF16),
        vmem((WIDTH, WIDTH), BF16),
        vmem((SEQ, ROWS, 3 * HEAD), F32),
        vmem((ROWS, WIDTH), F32),
        vmem((ROWS, WIDTH), BF16),
        vmem((ROWS, WIDTH), F32),
        vmem((ROWS, WIDTH), BF16),
        vmem((SEQ, ROWS, 3 * HEAD), BF16),
        vmem((SEQ, ROWS, 3 * HEAD), BF16),
        vmem((SEQ, ROWS, HEAD), BF16),
        vmem((LEN, HEAD), BF16),
        vmem((LEN, HEAD), BF16),
        vmem((LEN, HEAD), BF16),
        vmem((LEN, HEAD), BF16),
        vmem((LEN, LEN), F32),
        vmem((8, 8 * PACKS, HEAD), jnp.int32),
        vmem((8, 64 * PACKS, HEAD), jnp.int32),
        vmem((LEN, LEN), F32),
        vmem((LEN, LEN), BF16),
        vmem((LEN, LEN), BF16),
        vmem((LEN, HEAD), F32),
        vmem((8, LEN // 2), F32),
        vmem((SEQ, 8, LEN // 2), F32),
        vmem((LEN, HEAD), BF16),
        vmem((LEN, HEAD), F32),
        vmem((LEN, HEAD), BF16),
        vmem((HEAD, LEN), BF16),
        vmem((HEAD, LEN), BF16),
        vmem((SEQ, ROWS, HEAD), BF16),
        vmem((SEQ, ROWS, HEAD), BF16),
        vmem((LEN, 3 * HEAD), BF16),
        vmem((SEQ, ROWS, 3 * HEAD), BF16),
        vmem((SEQ, ROWS, 3 * HEAD), BF16),
        vmem((ROWS, WIDTH), BF16),
        vmem((ROWS, WIDTH), BF16),
        vmem((ROWS, WIDTH), BF16),
        vmem((ROWS, WIDTH), F32),
        vmem((8, ROWS, WIDTH), BF16),
        vmem((8, ROWS, HEAD), BF16),
        vmem((HEAD, 8 * ROWS), BF16),
        vmem((16, HALF, HEAD), BF16),
        vmem((15, HALF, HEAD), BF16),
        vmem((8, 8, HEAD), F32),
        vmem((8, 8, HEAD), F32),
        vmem((16, 8, HEAD), F32),
        vmem((8, 8, HEAD), F32),
        pltpu.SMEM((SEQ, BUCKETS), F32),
        pltpu.SMEM((1, 4), jnp.int32),
        vmem((1, LEN), jnp.int32),
        vmem((ROWS, WIDTH), BF16),
        vmem((ROWS, WIDTH), BF16),
        dma((2,)),
        dma((3,)),
        dma((12,)),
        dma,
        dma((7,)),
        dma,
        dma,
        dma,
        dma,
        dma,
        dma,
        dma,
        dma((7,)),
        dma,
        dma,
        dma,
        dma,
        dma,
        dma,
        dma,
        dma,
        dma,
        dma,
        dma,
        dma,
        dma,
        dma,
        dma,
        dma,
        dma,
        dma,
    ]
    hbm = pl.BlockSpec(memory_space=pl.ANY)
    local = pl.BlockSpec(memory_space=pltpu.VMEM)
    shapes = (
        jax.ShapeDtypeStruct((1, ROWS, WIDTH), BF16),
        jax.ShapeDtypeStruct((1, ROWS, WIDTH), BF16),
        jax.ShapeDtypeStruct((8, WIDTH), F32),
        jax.ShapeDtypeStruct((SEQ, BUCKETS), F32),
    )
    results = pl.pallas_call(
        kernel,
        out_shape=shapes,
        in_specs=[hbm] * 7,
        out_specs=(hbm, hbm, local, local),
        scratch_shapes=scratch,
        compiler_params=pltpu.CompilerParams(
            collective_id=0, has_side_effects=True, vmem_limit_bytes=60 * 2**20
        ),
    )(events, in_weight, out_weight, rab_table.T, lengths, stamps, cotangent)
    layer_out, input_grad, out_grad, bias_grad = pl.pallas_call(
        finish,
        out_shape=shapes,
        in_specs=[local] * 4,
        out_specs=(local,) * 4,
    )(*results)
    return (layer_out, input_grad, out_grad.T, bias_grad.T)


def solution(mesh):
    placed = (
        P("dp", "seq", None),
        P(),
        P(),
        P(),
        P("dp", None),
        P("dp", None),
        P("dp", "seq", None),
    )
    return jax.shard_map(
        body,
        mesh=mesh,
        in_specs=placed,
        out_specs=(P("dp", "seq", None), P("dp", "seq", None), P(None, ("dp", "seq")), P()),
        check_vma=False,
    )
```
